128 devices in a mesh: frame: 16 (over z, x_hi, core), seq: 8 (over x_lo, y).
Axes of the slice: x: 4 (x_hi: 2, x_lo: 2; x = x_hi * 2 + x_lo), y: 4, z: 4, core: 2. Of those that a mesh axis runs over, the one named last changes fastest.
Arguments:
- frames: bfloat16 [32, 2048, 1152], P('frame', 'seq'), may hold values from -6 to 6
- modulation: float32 [2, 3, 1152], replicated, may hold values from 0.5 to 1.5
- spatial_qkv: bfloat16 [1152, 3456], replicated, as said below
- spatial_out: bfloat16 [1152, 1152], replicated, may hold values from -0.1875 to 0.1875
- temporal_qkv: bfloat16 [1152, 3456], replicated, as said below
- temporal_out: bfloat16 [1152, 1152], replicated, may hold values from -0.1875 to 0.1875
- qk_gain: float32 [2, 2, 72], replicated, may hold values from 1.5 to 5
Outputs:
- block_out: bfloat16 [32, 2048, 1152], P('frame', 'seq')
The draws below stay inside these ranges and needn't reach their ends.
Inputs may be any that keep to these rules, and one draw needn't show every extreme that they name: `spatial_qkv`: entries of about 1/sqrt(1152) in size. `temporal_qkv`: entries of about 1/sqrt(1152) in size.
All inputs are finite; a program needn't handle non-finite values.
Results may differ from the reference program's by a relative error of at most 0.018.
Values may be sent and summed in bfloat16 or wider, within the bound.
A program may use at most 192 MiB of HBM per device.

```python
import jax
import jax.numpy as jnp
from jax import lax

HEADS = 16
HD = 72
D = 1152
FRAMES = 32
PATCHES = 2048


def projection_draw(key):
    first, second, third = jax.random.split(key, 3)
    query_part = jax.random.normal(first, (D, D), jnp.float32)
    value_part = jax.random.normal(third, (D, D), jnp.float32)
    key_part = jnp.sqrt(1.0) * jax.random.normal(second, (D, D), jnp.float32)
    whole = jnp.concatenate([query_part, key_part, value_part], axis=1) / jnp.sqrt(jnp.float32(D))
    return whole.astype(jnp.bfloat16)


def draw_spatial_qkv(key, part):
    key = jax.random.fold_in(key, 11)
    return projection_draw(key)


def draw_temporal_qkv(key, part):
    key = jax.random.fold_in(key, 23)
    return projection_draw(key)


def draw_qk_gain(key, part):
    key = jax.random.fold_in(key, 37)
    return jnp.exp(jax.random.uniform(key, (2, 2, HD), jnp.float32, jnp.log(1.5), jnp.log(3.0)))


def block_scale(own_key, dims, pieces, least, high):
    level = 1.0
    for dim, shards_of in pieces:
        heights = jax.random.uniform(jax.random.fold_in(jax.random.fold_in(own_key, 6), dim), (shards_of,), jnp.float32, least / len(pieces), high / len(pieces))
        level = level * jnp.repeat(jnp.exp(heights), dims[dim] // shards_of).reshape((-1,) + (1,) * (len(dims) - 1 - dim))
    return level


def gaussian(key, shape, scale, reach, cuts=(), kind=jnp.bfloat16):
    drawn = scale * jax.random.normal(key, shape, jnp.float32)
    if cuts:
        drawn = drawn * block_scale(key, shape, cuts, -0.22, 0.18)
    return jnp.clip(drawn, -reach, reach).astype(kind)


def setup_inputs(seed: int = 0) -> dict:
    seeds = jax.random.split(jax.random.key(seed), 8)
    frames = gaussian(seeds[0], (FRAMES, PATCHES, D), 1.0, 6.0, ((0, 16), (1, 8)))
    modulation = jnp.clip(jax.random.uniform(seeds[1], (2, 3, D), jnp.float32, 0.5, 1.5), 0.5, 1.5)
    spatial_qkv = draw_spatial_qkv(jax.random.fold_in(seeds[7], 71), 0)
    spatial_out = gaussian(seeds[3], (D, D), D ** -0.5, 0.1875)
    temporal_qkv = draw_temporal_qkv(jax.random.fold_in(seeds[7], 71), 0)
    temporal_out = gaussian(seeds[5], (D, D), D ** -0.5, 0.1875)
    qk_gain = draw_qk_gain(jax.random.fold_in(seeds[7], 71), 0)
    return {"frames": frames, "modulation": modulation, "spatial_qkv": spatial_qkv, "spatial_out": spatial_out, "temporal_qkv": temporal_qkv, "temporal_out": temporal_out, "qk_gain": qk_gain}


def modulate(stream, coefficients):
    values = stream.astype(jnp.float32)
    centre = lax.optimization_barrier(jnp.mean(values, axis=-1, keepdims=True))
    spread = lax.optimization_barrier(jnp.mean((values - centre) ** 2, axis=-1, keepdims=True))
    normal = (values - centre) * lax.rsqrt(spread + 1e-06)
    return (normal * (1.0 + coefficients[1]) + coefficients[0]).astype(jnp.bfloat16)

def qk_normalize(heads, gain):
    values = heads.astype(jnp.float32)
    factor = lax.rsqrt(lax.optimization_barrier(jnp.mean(values * values, axis=-1, keepdims=True)) + 1e-06)
    return (values * factor * gain).astype(jnp.bfloat16)

def project(normed, weight, gain):
    leading = normed.shape[:-1]
    width = weight.shape[0]
    projected = jnp.dot(normed.reshape(-1, width), weight, preferred_element_type=jnp.float32)
    projected = projected.astype(jnp.bfloat16).reshape(leading + (3, HEADS, HD))
    query_rows = qk_normalize(projected[..., 0, :, :], gain[0])
    key_rows = qk_normalize(projected[..., 1, :, :], gain[1])
    return jnp.stack([query_rows, key_rows, projected[..., 2, :, :]], axis=-3)

def attend(query_rows, key_rows, value_rows):
    scores = jnp.einsum('qhd,khd->hqk', query_rows.astype(jnp.float32), key_rows.astype(jnp.float32)) / jnp.sqrt(jnp.float32(HD))
    expo = jnp.exp(scores - lax.optimization_barrier(jnp.max(scores, axis=-1, keepdims=True)))
    denom = lax.optimization_barrier(jnp.sum(expo, axis=-1))
    weights = expo.astype(jnp.bfloat16)
    summed = jnp.einsum('hqk,khd->qhd', weights.astype(jnp.float32), value_rows.astype(jnp.float32))
    return (summed / jnp.transpose(denom)[:, :, None]).astype(jnp.bfloat16)

def residual(stream, attended, weight, gate):
    leading = stream.shape[:-1]
    width = weight.shape[0]
    branch = jnp.dot(attended.reshape(-1, width), weight, preferred_element_type=jnp.float32).reshape(leading + (width,))
    return (stream.astype(jnp.float32) + gate * branch).astype(jnp.bfloat16)

def reference(frames, modulation, spatial_qkv, spatial_out, temporal_qkv, temporal_out, qk_gain):
    packed = project(modulate(frames, modulation[0]), spatial_qkv, qk_gain[0])
    attended = lax.map(lambda block: attend(block[:, 0], block[:, 1], block[:, 2]), packed)
    stream_one = residual(frames, attended, spatial_out, modulation[0, 2])
    packed_two = project(modulate(stream_one, modulation[1]), temporal_qkv, qk_gain[1])
    attended_two = jax.vmap(attend, in_axes=(1, 1, 1), out_axes=1)(packed_two[:, :, 0], packed_two[:, :, 1], packed_two[:, :, 2])
    return residual(stream_one, attended_two, temporal_out, modulation[1, 2])
```

```python
import functools

import jax
import jax.numpy as jnp
from jax import lax
from jax.experimental import pallas as pl
from jax.experimental.pallas import tpu as pltpu
from jax.sharding import PartitionSpec as P

HEADS = 16
HD = 72
D = 1152
HALF = 8 * HD
MESH = pl.DeviceIdType.MESH
LOG2E = 1.4426950408889634
SCALE = LOG2E / 72.0 ** 0.5
F32 = jnp.float32
BF16 = jnp.bfloat16


def layer_norm(values, scale, shift):
    centre = jnp.mean(values, axis=-1, keepdims=True)
    moved = values - centre
    spread = jnp.mean(moved * moved, axis=-1, keepdims=True)
    normal = moved * lax.rsqrt(spread + 1e-06)
    return (normal * (1.0 + scale) + shift).astype(BF16)


def qk_normalize(heads, gain):
    factor = lax.rsqrt(jnp.mean(heads * heads, axis=1, keepdims=True) + 1e-06)
    return heads * factor * gain[None]


def pad_rows(heads, fill):
    n, _, tokens = heads.shape
    return jnp.concatenate([heads, jnp.full((n, 8, tokens), fill, F32)], axis=1)


def nt_dot(a, b):
    return lax.dot_general(a, b, (((1,), (1,)), ((), ())), preferred_element_type=F32)


def tn_dot(a, b):
    return lax.dot_general(a, b, (((0,), (0,)), ((), ())), preferred_element_type=F32)


def block_kernel(frames, modulation_in, gains_in, w_qkv, w_out, w_qkv_two, w_out_two, home,
                 modulation, gains_raw, gains, xbuf, raw, wt, wt_two, wo, wo_two, q_t, k_rows, v_t, o_t, att, att2, fr2, res, perm, bias,
                 m_sem, w_sem, x_send, x_recv, x_fwd, kv_send, kv_recv, a_send, a_recv, f_send, f_recv, r_send, r_recv, stage_two, stage_three,
                 *, exact):
    f_me = lax.axis_index("frame")
    s_me = lax.axis_index("seq")
    group, core = f_me // 2, f_me % 2
    x_lo, y = s_me // 4, s_me % 4
    primary = x_lo == core
    local = primary & (y // 2 == core)
    partner = 2 * group + 1 - core
    other_x = 4 * (1 - x_lo) + y

    def raw_copy(part):
        return pltpu.make_async_copy(
            w_qkv.at[:, pl.ds(pl.multiple_of(part * D + x_lo * 512, 128), 640)],
            raw.at[part, :, pl.ds(0, 640)], w_sem.at[part])

    def raw_copy_two(part):
        return pltpu.make_async_copy(w_qkv_two.at[:, pl.ds(pl.multiple_of(part * D, 128), D)], raw.at[part], w_sem.at[part])

    small_copies = [pltpu.make_async_copy(modulation_in, modulation, m_sem.at[0]),
                    pltpu.make_async_copy(gains_in, gains_raw, m_sem.at[1])]
    out_copies = [pltpu.make_async_copy(w_out, wo, w_sem.at[3]), pltpu.make_async_copy(w_out_two, wo_two, w_sem.at[4])]

    barrier = pltpu.get_barrier_semaphore()

    def column_mate(n):
        step = n + 1
        return (2 * group + lax.rem(core + step, 2), 4 * x_lo + lax.rem(y + step // 2, 4))

    def group_mate(n):
        return (lax.rem(f_me + 2 * (n + 1), 16), s_me)

    def tell(n, sem, mate):
        pl.semaphore_signal(sem, inc=1, device_id=mate(n), device_id_type=MESH)

    for n in range(7):
        tell(n, barrier, column_mate)
    for n in range(7):
        tell(n, barrier, group_mate)
    pl.semaphore_signal(barrier, inc=1, device_id=(f_me, other_x), device_id_type=MESH)
    for part in range(3):
        raw_copy(part).start()
    pl.semaphore_wait(barrier, 15)

    def send(i):
        return pltpu.make_async_remote_copy(
            src_ref=frames.at[i], dst_ref=xbuf.at[y], send_sem=x_send.at[i], recv_sem=x_recv.at[y],
            device_id=(2 * group + x_lo, 4 * x_lo + 2 * core + i), device_id_type=MESH)

    def forward(slot):
        return pltpu.make_async_remote_copy(
            src_ref=xbuf.at[slot], dst_ref=xbuf.at[slot], send_sem=x_fwd.at[slot], recv_sem=x_recv.at[slot],
            device_id=(f_me, other_x), device_id_type=MESH)

    def is_self(i):
        return primary & (2 * core + i == y)

    def is_far(i):
        return lax.rem(2 * core + i + 4 - y, 4) == 2

    for i in range(2):
        @pl.when(jnp.logical_not(is_self(i)) & jnp.logical_not(is_far(i)))
        def _(i=i):
            send(i).start()

        @pl.when(is_self(i))
        def _(i=i):
            pltpu.make_async_copy(frames.at[i], xbuf.at[y], x_recv.at[y]).start()

    for n in range(7):
        tell(n, stage_two, group_mate)
    for copy in small_copies:
        copy.start()
    for copy in out_copies:
        copy.start()

    def receive(slot):
        pltpu.make_async_copy(frames.at[0], xbuf.at[slot], x_recv.at[slot]).wait()

        @pl.when(primary)
        def _():
            forward(slot).start()

    receive(y)
    for copy in small_copies:
        copy.wait()
    pl.semaphore_wait(stage_two, 7)
    pl.semaphore_signal(stage_three, inc=1, device_id=(f_me, other_x), device_id_type=MESH)
    diagonal = lax.broadcasted_iota(jnp.int32, (HD, HD), 0) == lax.broadcasted_iota(jnp.int32, (HD, HD), 1)
    for layer in range(2):
        for which in range(2):
            gains[layer, which] = jnp.sum(
                jnp.where(diagonal, gains_raw[layer, which:which + 1, :], 0.0), axis=1, keepdims=True)
    for part in range(3):
        raw_copy(part).wait()
        wt[part] = raw[part, :, :640].T
        raw_copy_two(part).start()

    scale, shift = modulation[0, 1:2, :], modulation[0, 0:1, :]
    weight_rows = pl.ds(pl.multiple_of(x_lo * 64, 64), HALF)

    def k_copy(slot):
        cols = pl.ds(pl.multiple_of(core * 1024 + slot * 256, 256), 256)
        return pltpu.make_async_remote_copy(
            src_ref=k_rows.at[:, cols], dst_ref=k_rows.at[:, cols], send_sem=kv_send.at[0, slot],
            recv_sem=kv_recv.at[0, slot], device_id=(partner, s_me), device_id_type=MESH)

    def v_copy(slot):
        cols = pl.ds(pl.multiple_of(core * 1024 + slot * 256, 256), 256)
        return pltpu.make_async_remote_copy(
            src_ref=v_t.at[:, :, cols], dst_ref=v_t.at[:, :, cols], send_sem=kv_send.at[1, slot],
            recv_sem=kv_recv.at[1, slot], device_id=(partner, s_me), device_id_type=MESH)

    def kv_wait(slot):
        cols = pl.ds(pl.multiple_of((1 - core) * 1024 + slot * 256, 256), 256)
        pltpu.make_async_copy(k_rows.at[:, cols], k_rows.at[:, cols], kv_recv.at[0, slot]).wait()
        pltpu.make_async_copy(v_t.at[:, :, cols], v_t.at[:, :, cols], kv_recv.at[1, slot]).wait()

    def place(slot):
        far = lax.rem(slot + 4 - y, 4)
        return 2 * lax.rem(far, 2) + far // 2

    def work(slot):
        normed = layer_norm(xbuf[slot].astype(F32), scale, shift)
        here = pl.ds(pl.multiple_of(place(slot) * 256, 256), 256)
        cols = pl.ds(pl.multiple_of(core * 1024 + slot * 256, 256), 256)

        def projected(part):
            return nt_dot(wt[part, weight_rows, :], normed).astype(BF16).astype(F32).reshape(8, HD, 256)

        keys = pad_rows(qk_normalize(projected(1), gains[0, 1]), 1.0)
        for h in range(8):
            k_rows[h, cols, :] = keys[h].T.astype(BF16)
        k_copy(slot).start()
        v_t[:, :, cols] = pad_rows(projected(2), 1.0).astype(BF16)
        v_copy(slot).start()
        q_t[:, :, here] = pad_rows(qk_normalize(projected(0), gains[0, 0]), -6.0).astype(BF16)

    work(y)

    for i in range(2):
        @pl.when(is_far(i))
        def _(i=i):
            send(1 - i).wait_send()
            send(i).start()

    def chunk(n, carry):
        slot = lax.rem(y + n + (n // 2) * (1 - 2 * lax.rem(n, 2)), 4)
        receive(slot)
        raw_copy_two(n - 1).wait()
        wt_two[n - 1] = raw[n - 1].T
        work(slot)
        return carry

    lax.fori_loop(1, 4, chunk, 0)

    my_rows = pl.ds(pl.multiple_of(f_me * 16, 16), 16)

    def near(n):
        step = 15 - n
        z = lax.rem(f_me // 4 + lax.rem(step, 4), 4)
        x_hi = lax.rem(f_me // 2 + step // 4, 2)
        return 4 * z + 2 * x_hi + lax.rem(core + step // 8, 2)

    def send_frame(n, carry):
        other = near(n)
        rows = pl.ds(pl.multiple_of(other * 16, 16), 16)
        pltpu.make_async_remote_copy(
            src_ref=frames.at[:, rows], dst_ref=fr2.at[pl.ds(2 * f_me, 2)], send_sem=f_send, recv_sem=f_recv,
            device_id=(other, s_me), device_id_type=MESH).start()
        return carry

    pl.semaphore_wait(stage_three, 1)
    lax.fori_loop(0, 15, send_frame, 0)
    pltpu.make_async_copy(frames.at[:, my_rows], fr2.at[pl.ds(2 * f_me, 2)], f_recv).start()

    row = lax.broadcasted_iota(jnp.int32, (512, 512), 0)
    column = lax.broadcasted_iota(jnp.int32, (512, 512), 1)
    perm[...] = jnp.where(column == (row & 31) * 16 + (row >> 5), 1.0, 0.0).astype(BF16)
    row = lax.broadcasted_iota(jnp.int32, (256, 256), 0)
    column = lax.broadcasted_iota(jnp.int32, (256, 256), 1)
    bias[...] = jnp.where((row >> 5) == (column >> 5), 0.0, -1e30)

    for slot in range(4):
        kv_wait(slot)

    frame = 4 * group + y

    def finish(summed):
        return summed[:HD] / summed[HD:HD + 1]

    def attend(block):
        cols = slice(block * 512, block * 512 + 512)

        def head(h, carry):
            scores = jnp.dot(k_rows[h], q_t[h, :, cols], preferred_element_type=F32)
            if exact:
                scores = scores - jnp.max(scores, axis=0, keepdims=True)
            weights = jnp.exp2(scores * SCALE).astype(BF16)
            o_t[h, :, cols] = finish(jnp.dot(v_t[h], weights, preferred_element_type=F32))
            return carry

        lax.fori_loop(0, 8, head, 0)
        for part in range(4):
            rows = slice(block * 512 + part * 128, block * 512 + part * 128 + 128)
            att[rows, :] = o_t[:, :, rows].reshape(HALF, 128).T.astype(BF16)

        def send_att(n, carry):
            i = lax.rem(y + block + 2 * lax.rem(n, 2), 4)
            owner = near(n // 2)
            rows = pl.ds(pl.multiple_of(512 * block + 256 * lax.rem(n, 2) + owner * 16, 16), 16)
            mine = (owner == f_me) & (4 * core + i == s_me)

            @pl.when(jnp.logical_not(mine))
            def _():
                pltpu.make_async_remote_copy(
                    src_ref=att.at[rows], dst_ref=att2.at[x_lo, frame], send_sem=a_send, recv_sem=a_recv,
                    device_id=(owner, 4 * core + i), device_id_type=MESH).start()

            @pl.when(mine)
            def _():
                pltpu.make_async_copy(att.at[rows], att2.at[x_lo, frame], a_recv).start()
            return carry

        lax.fori_loop(0, 32, send_att, 0)

    for block in range(2):
        attend(block)

    for i in range(2):
        @pl.when(jnp.logical_not(is_self(i)) & jnp.logical_not(is_far(1 - i)))
        def _(i=i):
            send(i).wait_send()

    @pl.when(primary)
    def _():
        for slot in range(4):
            forward(slot).wait_send()

    for slot in range(4):
        k_copy(slot).wait_send()
        v_copy(slot).wait_send()
    for copy in out_copies:
        copy.wait()
    pltpu.make_async_copy(fr2, fr2, f_recv).wait()
    pltpu.make_async_copy(att2, att2, a_recv).wait()

    branch = jnp.dot(att2[0].reshape(512, HALF), wo[:HALF], preferred_element_type=F32)
    branch = branch + jnp.dot(att2[1].reshape(512, HALF), wo[HALF:], preferred_element_type=F32)
    stream = (fr2[...].reshape(512, D).astype(F32) + modulation[0, 2:3, :] * branch).astype(BF16)
    fr2[...] = stream.reshape(32, 16, D)
    normed = layer_norm(stream.astype(F32), modulation[1, 1:2, :], modulation[1, 0:1, :])
    normed = jnp.dot(perm[...], normed, preferred_element_type=F32).astype(BF16)

    def projected_two(part):
        return nt_dot(wt_two[part], normed).astype(BF16).astype(F32).reshape(HEADS, HD, 512)

    keys = pad_rows(qk_normalize(projected_two(1), gains[1, 1]), 1.0)
    for h in range(HEADS):
        k_rows[h // 2, pl.ds(512 * (h % 2), 512), :] = keys[h].T.astype(BF16)
    queries = pad_rows(qk_normalize(projected_two(0), gains[1, 0]), -6.0).astype(BF16)
    values = pad_rows(projected_two(2), 1.0).astype(BF16)
    for h in range(HEADS):
        q_t[h // 2, :, pl.ds(512 * (h % 2), 512)] = queries[h]
        v_t[h // 2, :, pl.ds(512 * (h % 2), 512)] = values[h]

    def head_pair(h, carry):
        for part in range(4):
            cols = slice(part * 256, part * 256 + 256)
            scores = jnp.dot(k_rows[h, cols, :], q_t[h, :, cols], preferred_element_type=F32) + bias[...]
            top = jnp.max(scores, axis=0, keepdims=True)
            weights = jnp.exp2((scores - top) * SCALE).astype(BF16)
            o_t[h, :, cols] = finish(jnp.dot(v_t[h, :, cols], weights, preferred_element_type=F32))
        return carry

    lax.fori_loop(0, 8, head_pair, 0)
    attended = jnp.concatenate([o_t[h // 2, :, 512 * (h % 2):512 * (h % 2) + 512] for h in range(HEADS)], axis=0)
    attended = jnp.dot(attended.astype(BF16), perm[...], preferred_element_type=F32).astype(BF16)
    xbuf_rows = attended.T

    for part in range(4):
        xbuf[part // 2, pl.ds(128 * (part % 2), 128), :] = xbuf_rows[128 * part:128 * part + 128]

    def last(n, carry):
        quarter = lax.rem(f_me // 4 + 2 + n + n // 2 * (1 - 2 * lax.rem(n, 2)), 4)
        rows = xbuf[quarter // 2, pl.ds(pl.multiple_of(128 * lax.rem(quarter, 2), 128), 128), :]
        branch_two = jnp.dot(rows, wo_two[...], preferred_element_type=F32)
        eight = pl.ds(8 * quarter, 8)
        result = fr2[eight].reshape(128, D).astype(F32) + modulation[1, 2:3, :] * branch_two
        res[eight] = result.astype(BF16).reshape(8, 16, D)
        for j in range(4):
            other = 4 * quarter + j

            @pl.when(other != f_me)
            def _(other=other):
                pltpu.make_async_remote_copy(
                    src_ref=res.at[pl.ds(2 * other, 2)], dst_ref=home.at[:, my_rows], send_sem=r_send, recv_sem=r_recv,
                    device_id=(other, s_me), device_id_type=MESH).start()

            @pl.when(other == f_me)
            def _(other=other):
                pltpu.make_async_copy(res.at[pl.ds(2 * other, 2)], home.at[:, my_rows], r_recv).start()
        return carry

    lax.fori_loop(0, 4, last, 0)

    @pl.when(primary)
    def _():
        part = att.at[pl.ds(0, 1008)]
        pltpu.make_async_copy(part, part, a_send).wait()

    @pl.when(jnp.logical_not(primary))
    def _():
        pltpu.make_async_copy(att, att, a_send).wait()
    most = fr2.at[pl.ds(0, 30)]
    pltpu.make_async_copy(most, most, f_send).wait()
    most = res.at[pl.ds(0, 30)]
    pltpu.make_async_copy(most, most, r_send).wait()
    pltpu.make_async_copy(home, home, r_recv).wait()


def block_call(exact, frames, modulation, gains, w_qkv, w_out, w_qkv_two, w_out_two):
    anywhere = pl.BlockSpec(memory_space=pl.ANY)
    dma = pltpu.SemaphoreType.DMA
    return pl.pallas_call(
        functools.partial(block_kernel, exact=exact),
        out_shape=jax.ShapeDtypeStruct((2, 256, D), BF16),
        in_specs=[anywhere, anywhere, anywhere, anywhere, anywhere, anywhere, anywhere],
        out_specs=anywhere,
        scratch_shapes=[
            pltpu.VMEM((2, 3, D), F32),
            pltpu.VMEM((2, 2, HD), F32),
            pltpu.VMEM((2, 2, HD, 1), F32),
            pltpu.VMEM((4, 256, D), BF16),
            pltpu.VMEM((3, D, D), BF16),
            pltpu.VMEM((3, 640, D), BF16),
            pltpu.VMEM((3, D, D), BF16),
            pltpu.VMEM((D, D), BF16),
            pltpu.VMEM((D, D), BF16),
            pltpu.VMEM((8, 80, 1024), BF16),
            pltpu.VMEM((8, 2048, 80), BF16),
            pltpu.VMEM((8, 80, 2048), BF16),
            pltpu.VMEM((8, HD, 1024), F32),
            pltpu.VMEM((1024, HALF), BF16),
            pltpu.VMEM((2, 32, 16, HALF), BF16),
            pltpu.VMEM((32, 16, D), BF16),
            pltpu.VMEM((32, 16, D), BF16),
            pltpu.VMEM((512, 512), BF16),
            pltpu.VMEM((256, 256), F32),
            dma((2,)), dma((5,)), dma((2,)), dma((4,)), dma((4,)), dma((2, 4)), dma((2, 4)),
            dma, dma, dma, dma, dma, dma, pltpu.SemaphoreType.REGULAR, pltpu.SemaphoreType.REGULAR,
        ],
        compiler_params=pltpu.CompilerParams(
            collective_id=1 if exact else 0, has_side_effects=True, vmem_limit_bytes=60 << 20),
        name="block_exact" if exact else "block",
    )(frames, modulation, gains, w_qkv, w_out, w_qkv_two, w_out_two)


def body(frames, modulation, spatial_qkv, spatial_out, temporal_qkv, temporal_out, qk_gain):
    largest = 72.0 * SCALE * jnp.max(jnp.abs(qk_gain[0, 0] * qk_gain[0, 1]))
    return lax.cond(
        largest <= 115.0, functools.partial(block_call, False), functools.partial(block_call, True),
        frames, modulation, qk_gain, spatial_qkv, spatial_out, temporal_qkv, temporal_out)


def solution(mesh):
    in_specs = (P("frame", "seq", None), P(), P(), P(), P(), P(), P())
    out_specs = P("frame", "seq", None)
    return jax.shard_map(body, mesh=mesh, in_specs=in_specs, out_specs=out_specs, check_vma=False)
```

```python
import functools

import jax
import jax.numpy as jnp
from jax import lax
from jax.experimental import pallas as pl
from jax.experimental.pallas import tpu as pltpu
from jax.sharding import PartitionSpec as P

HEADS = 16
HD = 72
D = 1152
HALF = 8 * HD
MESH = pl.DeviceIdType.MESH
LOG2E = 1.4426950408889634
SCALE = LOG2E / 72.0 ** 0.5
F32 = jnp.float32
BF16 = jnp.bfloat16


def layer_norm(values, scale, shift):
    centre = jnp.mean(values, axis=-1, keepdims=True)
    moved = values - centre
    spread = jnp.mean(moved * moved, axis=-1, keepdims=True)
    normal = moved * lax.rsqrt(spread + 1e-06)
    return (normal * (1.0 + scale) + shift).astype(BF16)


def qk_normalize(heads, gain):
    factor = lax.rsqrt(jnp.mean(heads * heads, axis=1, keepdims=True) + 1e-06)
    return heads * factor * gain[None]


def pad_rows(heads, fill):
    n, _, tokens = heads.shape
    return jnp.concatenate([heads, jnp.full((n, 8, tokens), fill, F32)], axis=1)


def nt_dot(a, b):
    return lax.dot_general(a, b, (((1,), (1,)), ((), ())), preferred_element_type=F32)


def tn_dot(a, b):
    return lax.dot_general(a, b, (((0,), (0,)), ((), ())), preferred_element_type=F32)


def block_kernel(frames, modulation_in, gains_in, w_qkv, w_out, w_qkv_two, w_out_two, home,
                 modulation, gains_raw, gains, xbuf, raw, wt, wt_two, wo, wo_two, q_t, k_rows, v_t, o_t, att, att2, fr2, res, perm, bias,
                 m_sem, w_sem, x_send, x_recv, x_fwd, kv_send, kv_recv, a_send, a_recv, f_send, f_recv, r_send, r_recv, stage_two,
                 *, exact):
    f_me = lax.axis_index("frame")
    s_me = lax.axis_index("seq")
    group, core = f_me // 2, f_me % 2
    x_lo, y = s_me // 4, s_me % 4
    half = lax.rem(y, 2)
    frame = 4 * group + 2 * x_lo + y // 2
    partner = 2 * group + 1 - core
    mate_row = y + 1 - 2 * half
    same = x_lo == core

    def raw_copy(part):
        return pltpu.make_async_copy(
            w_qkv.at[:, pl.ds(pl.multiple_of(part * D + half * 512, 128), 640)],
            raw.at[part, :, pl.ds(0, 640)], w_sem.at[part])

    def raw_copy_two(part):
        return pltpu.make_async_copy(w_qkv_two.at[:, pl.ds(pl.multiple_of(part * D, 128), D)], raw.at[part], w_sem.at[part])

    small_copies = [pltpu.make_async_copy(modulation_in, modulation, m_sem.at[0]),
                    pltpu.make_async_copy(gains_in, gains_raw, m_sem.at[1])]
    out_copies = [pltpu.make_async_copy(w_out, wo, w_sem.at[3]), pltpu.make_async_copy(w_out_two, wo_two, w_sem.at[4])]

    barrier = pltpu.get_barrier_semaphore()

    def plane_mate(n):
        step = n + 1
        return (2 * group + lax.rem(core + lax.rem(step, 2), 2),
                4 * lax.rem(x_lo + lax.rem(step // 2, 2), 2) + lax.rem(y + step // 4, 4))

    def group_mate(n):
        return (lax.rem(f_me + 2 * (n + 1), 16), s_me)

    def tell(n, sem, mate):
        pl.semaphore_signal(sem, inc=1, device_id=mate(n), device_id_type=MESH)

    for n in range(15):
        tell(n, barrier, plane_mate)
    for n in range(7):
        tell(n, barrier, group_mate)
    for part in range(3):
        raw_copy(part).start()
    pl.semaphore_wait(barrier, 22)

    def across(i):
        return lax.rem(i + y // 2, 2)

    def send(i):
        return pltpu.make_async_remote_copy(
            src_ref=frames.at[i], dst_ref=xbuf.at[y], send_sem=x_send.at[i], recv_sem=x_recv.at[y],
            device_id=(2 * group + x_lo, 4 * core + y + across(i) * (3 - 2 * y)), device_id_type=MESH)

    def forward(slot):
        return pltpu.make_async_remote_copy(
            src_ref=xbuf.at[slot], dst_ref=xbuf.at[slot], send_sem=x_fwd.at[slot], recv_sem=x_recv.at[slot],
            device_id=(f_me, 4 * x_lo + mate_row), device_id_type=MESH)

    for i in range(2):
        @pl.when((across(i) == 0) & jnp.logical_not(same))
        def _(i=i):
            send(i).start()

        @pl.when((across(i) == 0) & same)
        def _(i=i):
            pltpu.make_async_copy(frames.at[i], xbuf.at[y], x_recv.at[y]).start()

        @pl.when((across(i) == 1) & same)
        def _(i=i):
            send(i).start()

    for n in range(7):
        tell(n, stage_two, group_mate)
    for copy in small_copies:
        copy.start()
    for copy in out_copies:
        copy.start()

    def receive(slot):
        pltpu.make_async_copy(frames.at[0], xbuf.at[slot], x_recv.at[slot]).wait()

    receive(y)
    forward(y).start()
    for copy in small_copies:
        copy.wait()
    diagonal = lax.broadcasted_iota(jnp.int32, (HD, HD), 0) == lax.broadcasted_iota(jnp.int32, (HD, HD), 1)
    for layer in range(2):
        for which in range(2):
            gains[layer, which] = jnp.sum(
                jnp.where(diagonal, gains_raw[layer, which:which + 1, :], 0.0), axis=1, keepdims=True)
    for part in range(3):
        raw_copy(part).wait()
        wt[part] = raw[part, :, :640].T
        raw_copy_two(part).start()

    scale, shift = modulation[0, 1:2, :], modulation[0, 0:1, :]
    weight_rows = pl.ds(pl.multiple_of(half * 64, 64), HALF)

    def k_copy(slot):
        cols = pl.ds(pl.multiple_of(core * 1024 + slot * 256, 256), 256)
        return pltpu.make_async_remote_copy(
            src_ref=k_rows.at[:, cols], dst_ref=k_rows.at[:, cols], send_sem=kv_send.at[0, slot],
            recv_sem=kv_recv.at[0, slot], device_id=(partner, s_me), device_id_type=MESH)

    def v_copy(slot):
        cols = pl.ds(pl.multiple_of(core * 1024 + slot * 256, 256), 256)
        return pltpu.make_async_remote_copy(
            src_ref=v_t.at[:, :, cols], dst_ref=v_t.at[:, :, cols], send_sem=kv_send.at[1, slot],
            recv_sem=kv_recv.at[1, slot], device_id=(partner, s_me), device_id_type=MESH)

    def kv_wait(slot):
        cols = pl.ds(pl.multiple_of((1 - core) * 1024 + slot * 256, 256), 256)
        pltpu.make_async_copy(k_rows.at[:, cols], k_rows.at[:, cols], kv_recv.at[0, slot]).wait()
        pltpu.make_async_copy(v_t.at[:, :, cols], v_t.at[:, :, cols], kv_recv.at[1, slot]).wait()

    def work(slot):
        values = xbuf[slot].astype(F32).reshape(16, 2, 8, D)
        values = jnp.concatenate([values[:, 0].reshape(128, D), values[:, 1].reshape(128, D)], axis=0)
        normed = layer_norm(values, scale, shift)
        cols = pl.ds(pl.multiple_of(core * 1024 + slot * 256, 256), 256)

        def projected(part):
            return nt_dot(wt[part, weight_rows, :], normed).astype(BF16).astype(F32).reshape(8, HD, 256)

        keys = pad_rows(qk_normalize(projected(1), gains[0, 1]), 1.0)
        for h in range(8):
            k_rows[h, cols, :] = keys[h].T.astype(BF16)
        k_copy(slot).start()
        v_t[:, :, cols] = pad_rows(projected(2), 1.0).astype(BF16)
        v_copy(slot).start()
        queries = pad_rows(qk_normalize(projected(0), gains[0, 0]), -6.0).astype(BF16)
        q_t[:, :, pl.ds(pl.multiple_of(slot * 128, 128), 128)] = queries[:, :, :128]
        q_t[:, :, pl.ds(pl.multiple_of(512 + slot * 128, 128), 128)] = queries[:, :, 128:]

    work(y)

    for i in range(2):
        @pl.when((across(i) == 1) & jnp.logical_not(same))
        def _(i=i):
            send(1 - i).wait_send()
            send(i).start()

    pl.semaphore_wait(stage_two, 7)

    my_rows = pl.ds(pl.multiple_of(f_me * 16, 16), 16)

    def near(n):
        step = 15 - n
        z = lax.rem(f_me // 4 + lax.rem(step, 4), 4)
        x_hi = lax.rem(f_me // 2 + step // 4, 2)
        return 4 * z + 2 * x_hi + lax.rem(core + step // 8, 2)

    def send_frame(n, carry):
        other = near(n)
        rows = pl.ds(pl.multiple_of(other * 16, 16), 16)
        pltpu.make_async_remote_copy(
            src_ref=frames.at[:, rows], dst_ref=fr2.at[pl.ds(2 * f_me, 2)], send_sem=f_send, recv_sem=f_recv,
            device_id=(other, s_me), device_id_type=MESH).start()
        return carry

    lax.fori_loop(0, 15, send_frame, 0)
    pltpu.make_async_copy(frames.at[:, my_rows], fr2.at[pl.ds(2 * f_me, 2)], f_recv).start()

    def chunk(n, carry):
        row = y + (n // 2) * (mate_row - y)
        slot = row + lax.rem(n, 2) * (3 - 2 * row)
        receive(slot)

        @pl.when(n == 1)
        def _():
            forward(slot).start()

        raw_copy_two(n - 1).wait()
        wt_two[n - 1] = raw[n - 1].T
        work(slot)
        return carry

    lax.fori_loop(1, 4, chunk, 0)

    row = lax.broadcasted_iota(jnp.int32, (256, 256), 0)
    column = lax.broadcasted_iota(jnp.int32, (256, 256), 1)
    perm[...] = jnp.where(column == (row & 31) * 8 + (row >> 5), 1.0, 0.0).astype(BF16)
    bias[...] = jnp.where((row >> 5) == (column >> 5), 0.0, -1e30)

    for slot in range(4):
        kv_wait(slot)

    def finish(summed):
        return summed[:HD] / summed[HD:HD + 1]

    def attend(block):
        cols = slice(block * 512, block * 512 + 512)

        def head(h, carry):
            scores = jnp.dot(k_rows[h], q_t[h, :, cols], preferred_element_type=F32)
            if exact:
                scores = scores - jnp.max(scores, axis=0, keepdims=True)
            weights = jnp.exp2(scores * SCALE).astype(BF16)
            o_t[h, :, cols] = finish(jnp.dot(v_t[h], weights, preferred_element_type=F32))
            return carry

        lax.fori_loop(0, 8, head, 0)
        for part in range(4):
            cols = slice(block * 512 + part * 128, block * 512 + part * 128 + 128)
            rows = o_t[:, :, cols].reshape(HALF, 128).T.reshape(16, 8, HALF)
            att[block * 64 + part * 16:block * 64 + part * 16 + 16] = rows.astype(BF16)

        def send_att(n, carry):
            i = lax.rem(y + 2 * lax.rem(n, 2) + n // 32, 4)
            owner = near(lax.rem(n // 2, 16))
            block_ref = att.at[block * 64 + i * 16 + owner]
            mine = (owner == f_me) & (4 * core + i == s_me)

            @pl.when(jnp.logical_not(mine))
            def _():
                pltpu.make_async_remote_copy(
                    src_ref=block_ref, dst_ref=att2.at[block, half, frame], send_sem=a_send, recv_sem=a_recv.at[block],
                    device_id=(owner, 4 * core + i), device_id_type=MESH).start()

            @pl.when(mine)
            def _():
                pltpu.make_async_copy(block_ref, att2.at[block, half, frame], a_recv.at[block]).start()
            return carry

        lax.fori_loop(0, 64, send_att, 0)

    for block in range(2):
        attend(block)

    for i in range(2):
        @pl.when(across(i) == 1)
        def _(i=i):
            send(i).wait_send()

    forward(y).wait_send()
    forward(3 - y).wait_send()

    for slot in range(4):
        k_copy(slot).wait_send()
        v_copy(slot).wait_send()
    for copy in out_copies:
        copy.wait()
    pltpu.make_async_copy(fr2, fr2, f_recv).wait()

    def temporal(turn, carry):
        pltpu.make_async_copy(att2.at[turn], att2.at[turn], a_recv.at[turn]).wait()
        branch = jnp.zeros((256, D), F32)
        for hh in range(2):
            rows = att2[turn, hh].astype(F32).reshape(256, HALF).astype(BF16)
            branch = branch + jnp.dot(rows, wo[HALF * hh:HALF * hh + HALF], preferred_element_type=F32)
        rows = fr2[...].astype(F32).reshape(32, 2, 8, D)
        rows = jnp.where(turn == 0, rows[:, 0], rows[:, 1]).reshape(256, D)
        stream = (rows + modulation[0, 2:3, :] * branch).astype(BF16)
        normed = layer_norm(stream.astype(F32), modulation[1, 1:2, :], modulation[1, 0:1, :])
        normed = jnp.dot(perm[...], normed, preferred_element_type=F32).astype(BF16)

        def projected_two(part):
            return nt_dot(wt_two[part], normed).astype(BF16).astype(F32).reshape(HEADS, HD, 256)

        keys = pad_rows(qk_normalize(projected_two(1), gains[1, 1]), 1.0)
        queries = pad_rows(qk_normalize(projected_two(0), gains[1, 0]), -6.0).astype(BF16)
        values = pad_rows(projected_two(2), 1.0).astype(BF16)
        for h in range(HEADS):
            cols = pl.ds(256 * (h % 4), 256)
            k_rows[h // 4, cols, :] = keys[h].T.astype(BF16)
            q_t[h // 4, :, cols] = queries[h]
            v_t[h // 4, :, cols] = values[h]

        def four_heads(h, carry):
            parts = [slice(part * 256, part * 256 + 256) for part in range(4)]
            scores = [jnp.dot(k_rows[h, cols, :], q_t[h, :, cols], preferred_element_type=F32) for cols in parts]
            if exact:
                scores = [each - jnp.max(each + bias[...], axis=0, keepdims=True) for each in scores]
            weights = [jnp.exp2(each * SCALE + bias[...]).astype(BF16) for each in scores]
            summed = [jnp.dot(v_t[h, :, cols], each, preferred_element_type=F32) for cols, each in zip(parts, weights)]
            for cols, each in zip(parts, summed):
                o_t[h, :, cols] = finish(each)
            return carry

        lax.fori_loop(0, 4, four_heads, 0)
        attended = jnp.concatenate([o_t[h // 4, :, 256 * (h % 4):256 * (h % 4) + 256] for h in range(HEADS)], axis=0)
        attended = jnp.dot(attended.astype(BF16), perm[...], preferred_element_type=F32).astype(BF16)
        result = stream.astype(F32) + modulation[1, 2:3, :] * tn_dot(attended, wo_two[...])
        res[turn] = result.reshape(32, 8, D).astype(BF16)

        def send_home(n, carry):
            other = near(n)
            pltpu.make_async_remote_copy(
                src_ref=res.at[turn, pl.ds(2 * other, 2)], dst_ref=home.at[f_me, turn], send_sem=r_send, recv_sem=r_recv,
                device_id=(other, s_me), device_id_type=MESH).start()
            return carry

        lax.fori_loop(0, 15, send_home, 0)
        pltpu.make_async_copy(res.at[turn, pl.ds(2 * f_me, 2)], home.at[f_me, turn], r_recv).start()
        return carry

    lax.fori_loop(0, 2, temporal, 0)

    @pl.when(same)
    def _():
        part = att.at[pl.ds(0, 126)]
        pltpu.make_async_copy(part, part, a_send).wait()

    @pl.when(jnp.logical_not(same))
    def _():
        pltpu.make_async_copy(att, att, a_send).wait()
    most = fr2.at[pl.ds(0, 30)]
    pltpu.make_async_copy(most, most, f_send).wait()
    most = res.at[:, pl.ds(0, 30)]
    pltpu.make_async_copy(most, most, r_send).wait()
    pltpu.make_async_copy(home, home, r_recv).wait()


def block_call(exact, frames, modulation, gains, w_qkv, w_out, w_qkv_two, w_out_two):
    anywhere = pl.BlockSpec(memory_space=pl.ANY)
    dma = pltpu.SemaphoreType.DMA
    return pl.pallas_call(
        functools.partial(block_kernel, exact=exact),
        out_shape=jax.ShapeDtypeStruct((16, 2, 2, 8, D), BF16),
        in_specs=[anywhere, anywhere, anywhere, anywhere, anywhere, anywhere, anywhere],
        out_specs=anywhere,
        scratch_shapes=[
            pltpu.VMEM((2, 3, D), F32),
            pltpu.VMEM((2, 2, HD), F32),
            pltpu.VMEM((2, 2, HD, 1), F32),
            pltpu.VMEM((4, 256, D), BF16),
            pltpu.VMEM((3, D, D), BF16),
            pltpu.VMEM((3, 640, D), BF16),
            pltpu.VMEM((3, D, D), BF16),
            pltpu.VMEM((D, D), BF16),
            pltpu.VMEM((D, D), BF16),
            pltpu.VMEM((8, 80, 1024), BF16),
            pltpu.VMEM((8, 2048, 80), BF16),
            pltpu.VMEM((8, 80, 2048), BF16),
            pltpu.VMEM((8, HD, 1024), F32),
            pltpu.VMEM((128, 8, HALF), BF16),
            pltpu.VMEM((2, 2, 32, 8, HALF), BF16),
            pltpu.VMEM((32, 16, D), BF16),
            pltpu.VMEM((2, 32, 8, D), BF16),
            pltpu.VMEM((256, 256), BF16),
            pltpu.VMEM((256, 256), F32),
            dma((2,)), dma((5,)), dma((2,)), dma((4,)), dma((4,)), dma((2, 4)), dma((2, 4)),
            dma, dma((2,)), dma, dma, dma, dma, pltpu.SemaphoreType.REGULAR,
        ],
        compiler_params=pltpu.CompilerParams(
            collective_id=1 if exact else 0, has_side_effects=True, vmem_limit_bytes=60 << 20),
        name="block_exact" if exact else "block",
    )(frames, modulation, gains, w_qkv, w_out, w_qkv_two, w_out_two)


def body(frames, modulation, spatial_qkv, spatial_out, temporal_qkv, temporal_out, qk_gain):
    largest = 72.0 * SCALE * jnp.max(jnp.abs(qk_gain[:, 0] * qk_gain[:, 1]))
    home = lax.cond(
        largest <= 115.0, functools.partial(block_call, False), functools.partial(block_call, True),
        frames, modulation, qk_gain, spatial_qkv, spatial_out, temporal_qkv, temporal_out)
    return jnp.transpose(home, (2, 0, 1, 3, 4)).reshape(2, 256, D)


def solution(mesh):
    in_specs = (P("frame", "seq", None), P(), P(), P(), P(), P(), P())
    out_specs = P("frame", "seq", None)
    return jax.shard_map(body, mesh=mesh, in_specs=in_specs, out_specs=out_specs, check_vma=False)
```

```python
import functools

import jax
import jax.numpy as jnp
from jax import lax
from jax.experimental import pallas as pl
from jax.experimental.pallas import tpu as pltpu
from jax.sharding import PartitionSpec as P

HEADS = 16
HD = 72
D = 1152
HALF = 8 * HD
MESH = pl.DeviceIdType.MESH
LOG2E = 1.4426950408889634
SCALE = LOG2E / 72.0 ** 0.5
F32 = jnp.float32
BF16 = jnp.bfloat16


def layer_norm(values, scale, shift):
    centre = jnp.mean(values, axis=-1, keepdims=True)
    moved = values - centre
    spread = jnp.mean(moved * moved, axis=-1, keepdims=True)
    normal = moved * lax.rsqrt(spread + 1e-06)
    return (normal * (1.0 + scale) + shift).astype(BF16)


def qk_normalize(heads, gain):
    factor = lax.rsqrt(jnp.mean(heads * heads, axis=1, keepdims=True) + 1e-06)
    return heads * factor * gain[None]


def pad_rows(heads, fill):
    n, _, tokens = heads.shape
    return jnp.concatenate([heads, jnp.full((n, 8, tokens), fill, F32)], axis=1)


def nt_dot(a, b):
    return lax.dot_general(a, b, (((1,), (1,)), ((), ())), preferred_element_type=F32)


def tn_dot(a, b):
    return lax.dot_general(a, b, (((0,), (0,)), ((), ())), preferred_element_type=F32)


def block_kernel(frames, modulation_in, gains_in, w_qkv, w_out, w_qkv_two, w_out_two, home,
                 modulation, gains_raw, gains, xbuf, raw, wt, wt_two, wo, wo_two, q_t, k_rows, v_t, o_t, att, att2, fr2, res, perm, bias,
                 m_sem, w_sem, x_send, x_recv, x_fwd, kv_send, kv_recv, a_send, a_recv, f_send, f_recv, r_send, r_recv, stages,
                 *, exact):
    f_me = lax.axis_index("frame")
    s_me = lax.axis_index("seq")
    group, core = f_me // 2, f_me % 2
    x_lo, y = s_me // 4, s_me % 4
    half = lax.rem(y, 2)
    frame = 4 * group + 2 * x_lo + y // 2
    partner = 2 * group + 1 - core
    mate_row = y + 1 - 2 * half
    same = x_lo == core

    def raw_copy(part):
        return pltpu.make_async_copy(
            w_qkv.at[:, pl.ds(pl.multiple_of(part * D + half * 512, 128), 640)],
            raw.at[part, :, pl.ds(0, 640)], w_sem.at[part])

    def raw_copy_two(part):
        return pltpu.make_async_copy(w_qkv_two.at[:, pl.ds(pl.multiple_of(part * D, 128), D)], raw.at[part], w_sem.at[part])

    small_copies = [pltpu.make_async_copy(modulation_in, modulation, m_sem.at[0]),
                    pltpu.make_async_copy(gains_in, gains_raw, m_sem.at[1])]
    out_copies = [pltpu.make_async_copy(w_out, wo, w_sem.at[3]), pltpu.make_async_copy(w_out_two, wo_two, w_sem.at[4])]

    barrier = pltpu.get_barrier_semaphore()

    def plane_mate(n):
        step = n + 1
        return (2 * group + lax.rem(core + lax.rem(step, 2), 2),
                4 * lax.rem(x_lo + lax.rem(step // 2, 2), 2) + lax.rem(y + step // 4, 4))

    above, below = (lax.rem(f_me + 4, 16), s_me), (lax.rem(f_me + 12, 16), s_me)
    beside = (f_me + 2 - 4 * lax.rem(f_me // 2, 2), 4 * (1 - x_lo) + y)

    def tell(sem, mate):
        pl.semaphore_signal(sem, inc=1, device_id=mate, device_id_type=MESH)

    for n in range(15):
        tell(barrier, plane_mate(n))
    for mate in (above, below, beside):
        tell(barrier, mate)
    for part in range(3):
        raw_copy(part).start()
    pl.semaphore_wait(barrier, 18)

    def across(i):
        return lax.rem(i + y // 2, 2)

    def send(i):
        return pltpu.make_async_remote_copy(
            src_ref=frames.at[i], dst_ref=xbuf.at[y], send_sem=x_send.at[i], recv_sem=x_recv.at[y],
            device_id=(2 * group + x_lo, 4 * core + y + across(i) * (3 - 2 * y)), device_id_type=MESH)

    def forward(slot):
        return pltpu.make_async_remote_copy(
            src_ref=xbuf.at[slot], dst_ref=xbuf.at[slot], send_sem=x_fwd.at[slot], recv_sem=x_recv.at[slot],
            device_id=(f_me, 4 * x_lo + mate_row), device_id_type=MESH)

    for i in range(2):
        @pl.when((across(i) == 0) & jnp.logical_not(same))
        def _(i=i):
            send(i).start()

        @pl.when((across(i) == 0) & same)
        def _(i=i):
            pltpu.make_async_copy(frames.at[i], xbuf.at[y], x_recv.at[y]).start()

        @pl.when((across(i) == 1) & same)
        def _(i=i):
            send(i).start()

    for mate in (above, below):
        tell(stages.at[0], mate)
    for copy in small_copies:
        copy.start()
    for copy in out_copies:
        copy.start()

    def receive(slot):
        pltpu.make_async_copy(frames.at[0], xbuf.at[slot], x_recv.at[slot]).wait()

    receive(y)
    forward(y).start()
    for copy in small_copies:
        copy.wait()
    diagonal = lax.broadcasted_iota(jnp.int32, (HD, HD), 0) == lax.broadcasted_iota(jnp.int32, (HD, HD), 1)
    for layer in range(2):
        for which in range(2):
            gains[layer, which] = jnp.sum(
                jnp.where(diagonal, gains_raw[layer, which:which + 1, :], 0.0), axis=1, keepdims=True)
    for part in range(3):
        raw_copy(part).wait()
        wt[part] = raw[part, :, :640].T
        raw_copy_two(part).start()

    scale, shift = modulation[1, 0:1, :], modulation[0, 0:1, :]
    weight_rows = pl.ds(pl.multiple_of(half * 64, 64), HALF)

    def row_of(n):
        row = y + (n // 2) * (mate_row - y)
        return row + lax.rem(n, 2) * (3 - 2 * row)

    pl.semaphore_wait(stages.at[0], 2)
    tell(stages.at[1], above)

    def k_copy(n):
        cols = pl.ds(pl.multiple_of(n * 512 + core * 256, 256), 256)
        return pltpu.make_async_remote_copy(
            src_ref=k_rows.at[:, cols], dst_ref=k_rows.at[:, cols], send_sem=kv_send.at[0, n],
            recv_sem=kv_recv.at[0, n], device_id=(partner, s_me), device_id_type=MESH)

    def v_copy(n):
        cols = pl.ds(pl.multiple_of(n * 512 + core * 256, 256), 256)
        return pltpu.make_async_remote_copy(
            src_ref=v_t.at[:, :, cols], dst_ref=v_t.at[:, :, cols], send_sem=kv_send.at[1, n],
            recv_sem=kv_recv.at[1, n], device_id=(partner, s_me), device_id_type=MESH)

    def kv_wait(n):
        cols = pl.ds(pl.multiple_of(n * 512 + (1 - core) * 256, 256), 256)
        pltpu.make_async_copy(k_rows.at[:, cols], k_rows.at[:, cols], kv_recv.at[0, n]).wait()
        pltpu.make_async_copy(v_t.at[:, :, cols], v_t.at[:, :, cols], kv_recv.at[1, n]).wait()

    def work(n):
        values = xbuf[row_of(n)].astype(F32).reshape(16, 2, 8, D)
        values = jnp.concatenate([values[:, 0].reshape(128, D), values[:, 1].reshape(128, D)], axis=0)
        normed = layer_norm(values, scale, shift)
        cols = pl.ds(pl.multiple_of(n * 512 + core * 256, 256), 256)

        def projected(part):
            return nt_dot(wt[part, weight_rows, :], normed).astype(BF16).astype(F32).reshape(8, HD, 256)

        keys = pad_rows(qk_normalize(projected(1), gains[0, 1]), 1.0)
        for h in range(8):
            k_rows[h, cols, :] = keys[h].T.astype(BF16)
        k_copy(n).start()
        v_t[:, :, cols] = pad_rows(projected(2), 1.0).astype(BF16)
        v_copy(n).start()
        queries = pad_rows(qk_normalize(projected(0), gains[0, 0]), -6.0).astype(BF16)
        q_t[:, :, pl.ds(pl.multiple_of(n * 128, 128), 128)] = queries[:, :, :128]
        q_t[:, :, pl.ds(pl.multiple_of(512 + n * 128, 128), 128)] = queries[:, :, 128:]

    work(0)
    pl.semaphore_wait(stages.at[1], 1)
    tell(stages.at[2], beside)

    for i in range(2):
        @pl.when((across(i) == 1) & jnp.logical_not(same))
        def _(i=i):
            send(1 - i).wait_send()
            send(i).start()


    my_rows = pl.ds(pl.multiple_of(f_me * 16, 16), 16)

    def near(n):
        step = 15 - n
        z = lax.rem(f_me // 4 + lax.rem(step, 4), 4)
        x_hi = lax.rem(f_me // 2 + step // 4, 2)
        return 4 * z + 2 * x_hi + lax.rem(core + step // 8, 2)

    def send_frame(n, carry):
        other = near(n)
        rows = pl.ds(pl.multiple_of(other * 16, 16), 16)
        pltpu.make_async_remote_copy(
            src_ref=frames.at[:, rows], dst_ref=fr2.at[pl.ds(2 * f_me, 2)], send_sem=f_send, recv_sem=f_recv,
            device_id=(other, s_me), device_id_type=MESH).start()
        return carry


    def chunk(n, carry):
        slot = row_of(n)
        receive(slot)

        @pl.when(n == 1)
        def _():
            forward(slot).start()

        work(n)
        raw_copy_two(n - 1).wait()
        wt_two[n - 1] = raw[n - 1].T
        return carry

    pl.semaphore_wait(stages.at[2], 1)
    lax.fori_loop(4, 8, send_frame, 0)
    lax.fori_loop(12, 15, send_frame, 0)
    lax.fori_loop(1, 3, chunk, 0)
    raw_copy_two(2).wait()
    wt_two[2] = raw[2].T

    row = lax.broadcasted_iota(jnp.int32, (256, 256), 0)
    column = lax.broadcasted_iota(jnp.int32, (256, 256), 1)
    perm[...] = jnp.where(column == (row & 31) * 8 + (row >> 5), 1.0, 0.0).astype(BF16)
    bias[...] = jnp.where((row >> 5) == (column >> 5), 0.0, -1e30)

    def finish(summed):
        return summed[:HD] / summed[HD:HD + 1]

    lax.fori_loop(0, 4, send_frame, 0)
    lax.fori_loop(8, 12, send_frame, 0)
    pltpu.make_async_copy(frames.at[:, my_rows], fr2.at[pl.ds(2 * f_me, 2)], f_recv).start()
    receive(row_of(3))
    work(3)
    for n in range(4):
        kv_wait(n)

    def attend(block):
        cols = slice(block * 512, block * 512 + 512)

        def head(h, carry):
            scores = jnp.dot(k_rows[h], q_t[h, :, cols], preferred_element_type=F32)
            if exact:
                scores = scores - jnp.max(scores, axis=0, keepdims=True)
            weights = jnp.exp2(scores * SCALE).astype(BF16)
            o_t[h, :, cols] = finish(jnp.dot(v_t[h], weights, preferred_element_type=F32))
            return carry

        lax.fori_loop(0, 8, head, 0)
        for part in range(4):
            cols = slice(block * 512 + part * 128, block * 512 + part * 128 + 128)
            rows = o_t[:, :, cols].reshape(HALF, 128).T.reshape(16, 8, HALF)
            att[block * 64 + part * 16:block * 64 + part * 16 + 16] = rows.astype(BF16)

        def send_att(n, carry):
            part = n // 32 + lax.rem(n, 2) * (3 - 2 * (n // 32))
            i = row_of(part)
            owner = near(lax.rem(n // 2, 16))
            block_ref = att.at[block * 64 + part * 16 + owner]
            mine = (owner == f_me) & (4 * core + i == s_me)

            @pl.when(jnp.logical_not(mine))
            def _():
                pltpu.make_async_remote_copy(
                    src_ref=block_ref, dst_ref=att2.at[block, half, frame], send_sem=a_send, recv_sem=a_recv.at[block],
                    device_id=(owner, 4 * core + i), device_id_type=MESH).start()

            @pl.when(mine)
            def _():
                pltpu.make_async_copy(block_ref, att2.at[block, half, frame], a_recv.at[block]).start()
            return carry

        lax.fori_loop(0, 64, send_att, 0)

    for block in range(2):
        attend(block)

    for i in range(2):
        @pl.when(across(i) == 1)
        def _(i=i):
            send(i).wait_send()

    forward(y).wait_send()
    forward(3 - y).wait_send()

    for slot in range(4):
        k_copy(slot).wait_send()
        v_copy(slot).wait_send()
    for copy in out_copies:
        copy.wait()
    pltpu.make_async_copy(fr2, fr2, f_recv).wait()

    def temporal(turn, carry):
        pltpu.make_async_copy(att2.at[turn], att2.at[turn], a_recv.at[turn]).wait()
        branch = jnp.zeros((256, D), F32)
        for hh in range(2):
            rows = att2[turn, hh].astype(F32).reshape(256, HALF).astype(BF16)
            branch = branch + jnp.dot(rows, wo[HALF * hh:HALF * hh + HALF], preferred_element_type=F32)
        rows = fr2[...].astype(F32).reshape(32, 2, 8, D)
        rows = jnp.where(turn == 0, rows[:, 0], rows[:, 1]).reshape(256, D)
        stream = (rows + modulation[2, 0:1, :] * branch).astype(BF16)
        normed = layer_norm(stream.astype(F32), modulation[1, 1:2, :], modulation[0, 1:2, :])
        normed = jnp.dot(perm[...], normed, preferred_element_type=F32).astype(BF16)

        def projected_two(part):
            return nt_dot(wt_two[part], normed).astype(BF16).astype(F32).reshape(HEADS, HD, 256)

        keys = pad_rows(qk_normalize(projected_two(1), gains[1, 1]), 1.0)
        queries = pad_rows(qk_normalize(projected_two(0), gains[1, 0]), -6.0).astype(BF16)
        values = pad_rows(projected_two(2), 1.0).astype(BF16)
        for h in range(HEADS):
            cols = pl.ds(256 * (h % 4), 256)
            k_rows[h // 4, cols, :] = keys[h].T.astype(BF16)
            q_t[h // 4, :, cols] = queries[h]
            v_t[h // 4, :, cols] = values[h]

        def four_heads(h, carry):
            parts = [slice(part * 256, part * 256 + 256) for part in range(4)]
            scores = [jnp.dot(k_rows[h, cols, :], q_t[h, :, cols], preferred_element_type=F32) for cols in parts]
            if exact:
                scores = [each - jnp.max(each + bias[...], axis=0, keepdims=True) for each in scores]
            weights = [jnp.exp2(each * SCALE + bias[...]).astype(BF16) for each in scores]
            summed = [jnp.dot(v_t[h, :, cols], each, preferred_element_type=F32) for cols, each in zip(parts, weights)]
            for cols, each in zip(parts, summed):
                o_t[h, :, cols] = finish(each)
            return carry

        lax.fori_loop(0, 4, four_heads, 0)
        attended = jnp.concatenate([o_t[h // 4, :, 256 * (h % 4):256 * (h % 4) + 256] for h in range(HEADS)], axis=0)
        attended = jnp.dot(attended.astype(BF16), perm[...], preferred_element_type=F32).astype(BF16)
        result = stream.astype(F32) + modulation[2, 1:2, :] * tn_dot(attended, wo_two[...])
        res[turn] = result.reshape(32, 8, D).astype(BF16)

        def send_home(n, carry):
            other = near(n)
            pltpu.make_async_remote_copy(
                src_ref=res.at[turn, pl.ds(2 * other, 2)], dst_ref=home.at[f_me, turn], send_sem=r_send, recv_sem=r_recv,
                device_id=(other, s_me), device_id_type=MESH).start()
            return carry

        lax.fori_loop(0, 15, send_home, 0)
        pltpu.make_async_copy(res.at[turn, pl.ds(2 * f_me, 2)], home.at[f_me, turn], r_recv).start()
        return carry

    lax.fori_loop(0, 2, temporal, 0)

    @pl.when(same)
    def _():
        part = att.at[pl.ds(0, 126)]
        pltpu.make_async_copy(part, part, a_send).wait()

    @pl.when(jnp.logical_not(same))
    def _():
        pltpu.make_async_copy(att, att, a_send).wait()
    most = fr2.at[pl.ds(0, 30)]
    pltpu.make_async_copy(most, most, f_send).wait()
    most = res.at[:, pl.ds(0, 30)]
    pltpu.make_async_copy(most, most, r_send).wait()
    pltpu.make_async_copy(home, home, r_recv).wait()


def block_call(exact, frames, modulation, gains, w_qkv, w_out, w_qkv_two, w_out_two):
    anywhere = pl.BlockSpec(memory_space=pl.ANY)
    dma = pltpu.SemaphoreType.DMA
    return pl.pallas_call(
        functools.partial(block_kernel, exact=exact),
        out_shape=jax.ShapeDtypeStruct((16, 2, 2, 8, D), BF16),
        in_specs=[anywhere, anywhere, anywhere, anywhere, anywhere, anywhere, anywhere],
        out_specs=anywhere,
        scratch_shapes=[
            pltpu.VMEM((3, 2, D), F32),
            pltpu.VMEM((2, 2, HD), F32),
            pltpu.VMEM((2, 2, HD, 1), F32),
            pltpu.VMEM((4, 256, D), BF16),
            pltpu.VMEM((3, D, D), BF16),
            pltpu.VMEM((3, 640, D), BF16),
            pltpu.VMEM((3, D, D), BF16),
            pltpu.VMEM((D, D), BF16),
            pltpu.VMEM((D, D), BF16),
            pltpu.VMEM((8, 80, 1024), BF16),
            pltpu.VMEM((8, 2048, 80), BF16),
            pltpu.VMEM((8, 80, 2048), BF16),
            pltpu.VMEM((8, HD, 1024), F32),
            pltpu.VMEM((128, 8, HALF), BF16),
            pltpu.VMEM((2, 2, 32, 8, HALF), BF16),
            pltpu.VMEM((32, 16, D), BF16),
            pltpu.VMEM((2, 32, 8, D), BF16),
            pltpu.VMEM((256, 256), BF16),
            pltpu.VMEM((256, 256), F32),
            dma((2,)), dma((5,)), dma((2,)), dma((4,)), dma((4,)), dma((2, 4)), dma((2, 4)),
            dma, dma((2,)), dma, dma, dma, dma, pltpu.SemaphoreType.REGULAR((3,)),
        ],
        compiler_params=pltpu.CompilerParams(
            collective_id=1 if exact else 0, has_side_effects=True, vmem_limit_bytes=60 << 20),
        name="block_exact" if exact else "block",
    )(frames, modulation, gains, w_qkv, w_out, w_qkv_two, w_out_two)


def body(frames, modulation, spatial_qkv, spatial_out, temporal_qkv, temporal_out, qk_gain):
    largest = jnp.max(jnp.abs(qk_gain[:, 0] * qk_gain[:, 1]))
    home = lax.cond(
        largest <= 115.0 / (72.0 * SCALE), functools.partial(block_call, False), functools.partial(block_call, True),
        frames, jnp.transpose(modulation, (1, 0, 2)), qk_gain, spatial_qkv, spatial_out, temporal_qkv, temporal_out)
    return jnp.transpose(home, (2, 0, 1, 3, 4)).reshape(2, 256, D)


def solution(mesh):
    in_specs = (P("frame", "seq", None), P(), P(), P(), P(), P(), P())
    out_specs = P("frame", "seq", None)
    return jax.shard_map(body, mesh=mesh, in_specs=in_specs, out_specs=out_specs, check_vma=False)
```

```python
import functools

import jax
import jax.numpy as jnp
from jax import lax
from jax.experimental import pallas as pl
from jax.experimental.pallas import tpu as pltpu
from jax.sharding import PartitionSpec as P

HEADS = 16
HD = 72
D = 1152
HALF = 8 * HD
MESH = pl.DeviceIdType.MESH
LOG2E = 1.4426950408889634
SCALE = LOG2E / 72.0 ** 0.5
F32 = jnp.float32
BF16 = jnp.bfloat16


def layer_norm(values, scale, shift):
    centre = jnp.mean(values, axis=-1, keepdims=True)
    moved = values - centre
    spread = jnp.mean(moved * moved, axis=-1, keepdims=True)
    normal = moved * lax.rsqrt(spread + 1e-06)
    return (normal * (1.0 + scale) + shift).astype(BF16)


def qk_normalize(heads, gain):
    factor = lax.rsqrt(jnp.mean(heads * heads, axis=1, keepdims=True) + 1e-06)
    return heads * factor * gain[None]


def pad_rows(heads, fill):
    n, _, tokens = heads.shape
    return jnp.concatenate([heads, jnp.full((n, 8, tokens), fill, F32)], axis=1)


def nt_dot(a, b):
    return lax.dot_general(a, b, (((1,), (1,)), ((), ())), preferred_element_type=F32)


def tn_dot(a, b):
    return lax.dot_general(a, b, (((0,), (0,)), ((), ())), preferred_element_type=F32)


def block_kernel(frames, modulation_in, gains_in, w_qkv, w_out, w_qkv_two, w_out_two, home,
                 modulation, gains_raw, gains, xbuf, raw, wt, wt_two, wo, wo_two, q_t, k_rows, v_t, o_t, att, att2, fr2, res, perm, bias,
                 m_sem, w_sem, x_send, x_recv, x_fwd, kv_send, kv_recv, a_send, a_recv, f_send, f_recv, r_send, r_recv, stages,
                 *, exact):
    f_me = lax.axis_index("frame")
    s_me = lax.axis_index("seq")
    group, core = f_me // 2, f_me % 2
    x_lo, y = s_me // 4, s_me % 4
    half = lax.rem(y, 2)
    frame = 4 * group + 2 * x_lo + y // 2
    partner = 2 * group + 1 - core
    mate_row = y + 1 - 2 * half
    same = x_lo == core

    def raw_copy(part):
        return pltpu.make_async_copy(
            w_qkv.at[:, pl.ds(pl.multiple_of(part * D + half * 512, 128), 640)],
            raw.at[part, :, pl.ds(0, 640)], w_sem.at[part])

    def raw_copy_two(part):
        return pltpu.make_async_copy(w_qkv_two.at[:, pl.ds(pl.multiple_of(part * D, 128), D)], raw.at[part], w_sem.at[part])

    small_copies = [pltpu.make_async_copy(modulation_in, modulation, m_sem.at[0]),
                    pltpu.make_async_copy(gains_in, gains_raw, m_sem.at[1])]
    out_copies = [pltpu.make_async_copy(w_out, wo, w_sem.at[3]), pltpu.make_async_copy(w_out_two, wo_two, w_sem.at[4])]

    barrier = pltpu.get_barrier_semaphore()

    def plane_mate(n):
        step = n + 1
        return (2 * group + lax.rem(core + lax.rem(step, 2), 2),
                4 * lax.rem(x_lo + lax.rem(step // 2, 2), 2) + lax.rem(y + step // 4, 4))

    above, below = (lax.rem(f_me + 4, 16), s_me), (lax.rem(f_me + 12, 16), s_me)
    beside = (f_me + 2 - 4 * lax.rem(f_me // 2, 2), 4 * (1 - x_lo) + y)

    def tell(sem, mate):
        pl.semaphore_signal(sem, inc=1, device_id=mate, device_id_type=MESH)

    for n in range(15):
        tell(barrier, plane_mate(n))
    for mate in (above, below, beside):
        tell(barrier, mate)
    for part in range(3):
        raw_copy(part).start()
    pl.semaphore_wait(barrier, 18)

    def across(i):
        return lax.rem(i + y // 2, 2)

    def send(i):
        return pltpu.make_async_remote_copy(
            src_ref=frames.at[i], dst_ref=xbuf.at[y], send_sem=x_send.at[i], recv_sem=x_recv.at[y],
            device_id=(2 * group + x_lo, 4 * core + y + across(i) * (3 - 2 * y)), device_id_type=MESH)

    def forward(slot):
        return pltpu.make_async_remote_copy(
            src_ref=xbuf.at[slot], dst_ref=xbuf.at[slot], send_sem=x_fwd.at[slot], recv_sem=x_recv.at[slot],
            device_id=(f_me, 4 * x_lo + mate_row), device_id_type=MESH)

    for i in range(2):
        @pl.when((across(i) == 0) & jnp.logical_not(same))
        def _(i=i):
            send(i).start()

        @pl.when((across(i) == 0) & same)
        def _(i=i):
            pltpu.make_async_copy(frames.at[i], xbuf.at[y], x_recv.at[y]).start()

        @pl.when((across(i) == 1) & same)
        def _(i=i):
            send(i).start()

    for mate in (above, below):
        tell(stages.at[0], mate)
    for copy in small_copies:
        copy.start()
    for copy in out_copies:
        copy.start()

    def receive(slot):
        pltpu.make_async_copy(frames.at[0], xbuf.at[slot], x_recv.at[slot]).wait()

    receive(y)
    forward(y).start()
    for i in range(2):
        @pl.when((across(i) == 1) & jnp.logical_not(same))
        def _(i=i):
            send(1 - i).wait_send()
            send(i).start()

    for copy in small_copies:
        copy.wait()
    diagonal = lax.broadcasted_iota(jnp.int32, (HD, HD), 0) == lax.broadcasted_iota(jnp.int32, (HD, HD), 1)
    for layer in range(2):
        for which in range(2):
            gains[layer, which] = jnp.sum(
                jnp.where(diagonal, gains_raw[layer, which:which + 1, :], 0.0), axis=1, keepdims=True)
    for part in range(3):
        raw_copy(part).wait()
        wt[part] = raw[part, :, :640].T
        raw_copy_two(part).start()

    scale, shift = modulation[1, 0:1, :], modulation[0, 0:1, :]
    weight_rows = pl.ds(pl.multiple_of(half * 64, 64), HALF)

    def row_of(n):
        row = y + (n // 2) * (mate_row - y)
        return row + lax.rem(n, 2) * (3 - 2 * row)

    pl.semaphore_wait(stages.at[0], 2)
    tell(stages.at[1], above)

    def k_copy(n):
        cols = pl.ds(pl.multiple_of(n * 512 + core * 256, 256), 256)
        return pltpu.make_async_remote_copy(
            src_ref=k_rows.at[:, cols], dst_ref=k_rows.at[:, cols], send_sem=kv_send.at[0, n],
            recv_sem=kv_recv.at[0, n], device_id=(partner, s_me), device_id_type=MESH)

    def v_copy(n):
        cols = pl.ds(pl.multiple_of(n * 512 + core * 256, 256), 256)
        return pltpu.make_async_remote_copy(
            src_ref=v_t.at[:, :, cols], dst_ref=v_t.at[:, :, cols], send_sem=kv_send.at[1, n],
            recv_sem=kv_recv.at[1, n], device_id=(partner, s_me), device_id_type=MESH)

    def kv_wait(n):
        cols = pl.ds(pl.multiple_of(n * 512 + (1 - core) * 256, 256), 256)
        pltpu.make_async_copy(k_rows.at[:, cols], k_rows.at[:, cols], kv_recv.at[0, n]).wait()
        pltpu.make_async_copy(v_t.at[:, :, cols], v_t.at[:, :, cols], kv_recv.at[1, n]).wait()

    def work(n):
        values = xbuf[row_of(n)].astype(F32).reshape(16, 2, 8, D)
        values = jnp.concatenate([values[:, 0].reshape(128, D), values[:, 1].reshape(128, D)], axis=0)
        normed = layer_norm(values, scale, shift)
        cols = pl.ds(pl.multiple_of(n * 512 + core * 256, 256), 256)

        def projected(part):
            return nt_dot(wt[part, weight_rows, :], normed).astype(BF16).astype(F32).reshape(8, HD, 256)

        keys = pad_rows(qk_normalize(projected(1), gains[0, 1]), 1.0)
        for h in range(8):
            k_rows[h, cols, :] = keys[h].T.astype(BF16)
        k_copy(n).start()
        v_t[:, :, cols] = pad_rows(projected(2), 1.0).astype(BF16)
        v_copy(n).start()
        queries = pad_rows(qk_normalize(projected(0), gains[0, 0]), -6.0).astype(BF16)
        q_t[:, :, pl.ds(pl.multiple_of(n * 128, 128), 128)] = queries[:, :, :128]
        q_t[:, :, pl.ds(pl.multiple_of(512 + n * 128, 128), 128)] = queries[:, :, 128:]

    work(0)
    pl.semaphore_wait(stages.at[1], 1)
    tell(stages.at[2], beside)


    my_rows = pl.ds(pl.multiple_of(f_me * 16, 16), 16)

    def near(n):
        step = 15 - n
        z = lax.rem(f_me // 4 + lax.rem(step, 4), 4)
        x_hi = lax.rem(f_me // 2 + step // 4, 2)
        return 4 * z + 2 * x_hi + lax.rem(core + step // 8, 2)

    def send_frame(n, carry):
        other = near(n)
        rows = pl.ds(pl.multiple_of(other * 16, 16), 16)
        pltpu.make_async_remote_copy(
            src_ref=frames.at[:, rows], dst_ref=fr2.at[pl.ds(2 * f_me, 2)], send_sem=f_send, recv_sem=f_recv,
            device_id=(other, s_me), device_id_type=MESH).start()
        return carry


    def chunk(n, carry):
        slot = row_of(n)
        receive(slot)

        @pl.when(n == 1)
        def _():
            forward(slot).start()

        work(n)
        raw_copy_two(n - 1).wait()
        wt_two[n - 1] = raw[n - 1].T
        return carry

    pl.semaphore_wait(stages.at[2], 1)
    lax.fori_loop(4, 8, send_frame, 0)
    lax.fori_loop(12, 15, send_frame, 0)
    lax.fori_loop(1, 3, chunk, 0)
    raw_copy_two(2).wait()
    wt_two[2] = raw[2].T

    row = lax.broadcasted_iota(jnp.int32, (256, 256), 0)
    column = lax.broadcasted_iota(jnp.int32, (256, 256), 1)
    perm[...] = jnp.where(column == (row & 31) * 8 + (row >> 5), 1.0, 0.0).astype(BF16)
    bias[...] = jnp.where((row >> 5) == (column >> 5), 0.0, -1e30)

    def finish(summed):
        return summed[:HD] / summed[HD:HD + 1]

    lax.fori_loop(0, 4, send_frame, 0)
    lax.fori_loop(8, 12, send_frame, 0)
    pltpu.make_async_copy(frames.at[:, my_rows], fr2.at[pl.ds(2 * f_me, 2)], f_recv).start()
    receive(row_of(3))
    work(3)
    for n in range(4):
        kv_wait(n)

    def attend(block):
        cols = slice(block * 512, block * 512 + 512)

        def head(h, carry):
            scores = jnp.dot(k_rows[h], q_t[h, :, cols], preferred_element_type=F32)
            if exact:
                scores = scores - jnp.max(scores, axis=0, keepdims=True)
            weights = jnp.exp2(scores * SCALE).astype(BF16)
            o_t[h, :, cols] = finish(jnp.dot(v_t[h], weights, preferred_element_type=F32))
            return carry

        lax.fori_loop(0, 8, head, 0)
        for part in range(4):
            cols = slice(block * 512 + part * 128, block * 512 + part * 128 + 128)
            rows = o_t[:, :, cols].reshape(HALF, 128).T.reshape(16, 8, HALF)
            att[block * 64 + part * 16:block * 64 + part * 16 + 16] = rows.astype(BF16)

        def send_att(n, carry):
            part = n // 32 + lax.rem(n, 2) * (3 - 2 * (n // 32))
            i = row_of(part)
            owner = near(lax.rem(n // 2, 16))
            block_ref = att.at[block * 64 + part * 16 + owner]
            mine = (owner == f_me) & (4 * core + i == s_me)

            @pl.when(jnp.logical_not(mine))
            def _():
                pltpu.make_async_remote_copy(
                    src_ref=block_ref, dst_ref=att2.at[block, half, frame], send_sem=a_send, recv_sem=a_recv.at[block],
                    device_id=(owner, 4 * core + i), device_id_type=MESH).start()

            @pl.when(mine)
            def _():
                pltpu.make_async_copy(block_ref, att2.at[block, half, frame], a_recv.at[block]).start()
            return carry

        lax.fori_loop(0, 64, send_att, 0)

    for block in range(2):
        attend(block)

    for i in range(2):
        @pl.when(across(i) == 1)
        def _(i=i):
            send(i).wait_send()

    forward(y).wait_send()
    forward(3 - y).wait_send()

    for slot in range(4):
        k_copy(slot).wait_send()
        v_copy(slot).wait_send()
    for copy in out_copies:
        copy.wait()
    pltpu.make_async_copy(fr2, fr2, f_recv).wait()

    def temporal(turn, carry):
        pltpu.make_async_copy(att2.at[turn], att2.at[turn], a_recv.at[turn]).wait()
        branch = jnp.zeros((256, D), F32)
        for hh in range(2):
            rows = att2[turn, hh].astype(F32).reshape(256, HALF).astype(BF16)
            branch = branch + jnp.dot(rows, wo[HALF * hh:HALF * hh + HALF], preferred_element_type=F32)
        rows = fr2[...].astype(F32).reshape(32, 2, 8, D)
        rows = jnp.where(turn == 0, rows[:, 0], rows[:, 1]).reshape(256, D)
        stream = (rows + modulation[2, 0:1, :] * branch).astype(BF16)
        normed = layer_norm(stream.astype(F32), modulation[1, 1:2, :], modulation[0, 1:2, :])
        normed = jnp.dot(perm[...], normed, preferred_element_type=F32).astype(BF16)

        def projected_two(part):
            return nt_dot(wt_two[part], normed).astype(BF16).astype(F32).reshape(HEADS, HD, 256)

        keys = pad_rows(qk_normalize(projected_two(1), gains[1, 1]), 1.0)
        queries = pad_rows(qk_normalize(projected_two(0), gains[1, 0]), -6.0).astype(BF16)
        values = pad_rows(projected_two(2), 1.0).astype(BF16)
        for h in range(HEADS):
            cols = pl.ds(256 * (h % 4), 256)
            k_rows[h // 4, cols, :] = keys[h].T.astype(BF16)
            q_t[h // 4, :, cols] = queries[h]
            v_t[h // 4, :, cols] = values[h]

        def four_heads(h, carry):
            parts = [slice(part * 256, part * 256 + 256) for part in range(4)]
            scores = [jnp.dot(k_rows[h, cols, :], q_t[h, :, cols], preferred_element_type=F32) for cols in parts]
            if exact:
                scores = [each - jnp.max(each + bias[...], axis=0, keepdims=True) for each in scores]
            weights = [jnp.exp2(each * SCALE + bias[...]).astype(BF16) for each in scores]
            summed = [jnp.dot(v_t[h, :, cols], each, preferred_element_type=F32) for cols, each in zip(parts, weights)]
            for cols, each in zip(parts, summed):
                o_t[h, :, cols] = finish(each)
            return carry

        lax.fori_loop(0, 4, four_heads, 0)
        attended = jnp.concatenate([o_t[h // 4, :, 256 * (h % 4):256 * (h % 4) + 256] for h in range(HEADS)], axis=0)
        attended = jnp.dot(attended.astype(BF16), perm[...], preferred_element_type=F32).astype(BF16)
        result = stream.astype(F32) + modulation[2, 1:2, :] * tn_dot(attended, wo_two[...])
        res[turn] = result.reshape(32, 8, D).astype(BF16)

        def send_home(n, carry):
            other = near(n)
            pltpu.make_async_remote_copy(
                src_ref=res.at[turn, pl.ds(2 * other, 2)], dst_ref=home.at[f_me, turn], send_sem=r_send, recv_sem=r_recv,
                device_id=(other, s_me), device_id_type=MESH).start()
            return carry

        lax.fori_loop(0, 15, send_home, 0)
        pltpu.make_async_copy(res.at[turn, pl.ds(2 * f_me, 2)], home.at[f_me, turn], r_recv).start()
        return carry

    lax.fori_loop(0, 2, temporal, 0)

    @pl.when(same)
    def _():
        part = att.at[pl.ds(0, 126)]
        pltpu.make_async_copy(part, part, a_send).wait()

    @pl.when(jnp.logical_not(same))
    def _():
        pltpu.make_async_copy(att, att, a_send).wait()
    most = fr2.at[pl.ds(0, 30)]
    pltpu.make_async_copy(most, most, f_send).wait()
    most = res.at[:, pl.ds(0, 30)]
    pltpu.make_async_copy(most, most, r_send).wait()
    pltpu.make_async_copy(home, home, r_recv).wait()


def block_call(exact, frames, modulation, gains, w_qkv, w_out, w_qkv_two, w_out_two):
    anywhere = pl.BlockSpec(memory_space=pl.ANY)
    dma = pltpu.SemaphoreType.DMA
    return pl.pallas_call(
        functools.partial(block_kernel, exact=exact),
        out_shape=jax.ShapeDtypeStruct((16, 2, 2, 8, D), BF16),
        in_specs=[anywhere, anywhere, anywhere, anywhere, anywhere, anywhere, anywhere],
        out_specs=anywhere,
        scratch_shapes=[
            pltpu.VMEM((3, 2, D), F32),
            pltpu.VMEM((2, 2, HD), F32),
            pltpu.VMEM((2, 2, HD, 1), F32),
            pltpu.VMEM((4, 256, D), BF16),
            pltpu.VMEM((3, D, D), BF16),
            pltpu.VMEM((3, 640, D), BF16),
            pltpu.VMEM((3, D, D), BF16),
            pltpu.VMEM((D, D), BF16),
            pltpu.VMEM((D, D), BF16),
            pltpu.VMEM((8, 80, 1024), BF16),
            pltpu.VMEM((8, 2048, 80), BF16),
            pltpu.VMEM((8, 80, 2048), BF16),
            pltpu.VMEM((8, HD, 1024), F32),
            pltpu.VMEM((128, 8, HALF), BF16),
            pltpu.VMEM((2, 2, 32, 8, HALF), BF16),
            pltpu.VMEM((32, 16, D), BF16),
            pltpu.VMEM((2, 32, 8, D), BF16),
            pltpu.VMEM((256, 256), BF16),
            pltpu.VMEM((256, 256), F32),
            dma((2,)), dma((5,)), dma((2,)), dma((4,)), dma((4,)), dma((2, 4)), dma((2, 4)),
            dma, dma((2,)), dma, dma, dma, dma, pltpu.SemaphoreType.REGULAR((3,)),
        ],
        compiler_params=pltpu.CompilerParams(
            collective_id=1 if exact else 0, has_side_effects=True, vmem_limit_bytes=60 << 20),
        name="block_exact" if exact else "block",
    )(frames, modulation, gains, w_qkv, w_out, w_qkv_two, w_out_two)


def body(frames, modulation, spatial_qkv, spatial_out, temporal_qkv, temporal_out, qk_gain):
    largest = jnp.max(jnp.abs(qk_gain[:, 0] * qk_gain[:, 1]))
    home = lax.cond(
        largest <= 115.0 / (72.0 * SCALE), functools.partial(block_call, False), functools.partial(block_call, True),
        frames, jnp.transpose(modulation, (1, 0, 2)), qk_gain, spatial_qkv, spatial_out, temporal_qkv, temporal_out)
    return jnp.transpose(home, (2, 0, 1, 3, 4)).reshape(2, 256, D)


def solution(mesh):
    in_specs = (P("frame", "seq", None), P(), P(), P(), P(), P(), P())
    out_specs = P("frame", "seq", None)
    return jax.shard_map(body, mesh=mesh, in_specs=in_specs, out_specs=out_specs, check_vma=False)
```

```python
import functools

import jax
import jax.numpy as jnp
from jax import lax
from jax.experimental import pallas as pl
from jax.experimental.pallas import tpu as pltpu
from jax.sharding import PartitionSpec as P

HEADS = 16
HD = 72
D = 1152
HALF = 8 * HD
MESH = pl.DeviceIdType.MESH
LOG2E = 1.4426950408889634
SCALE = LOG2E / 72.0 ** 0.5
F32 = jnp.float32
BF16 = jnp.bfloat16


def layer_norm(values, scale, shift):
    centre = jnp.mean(values, axis=-1, keepdims=True)
    moved = values - centre
    spread = jnp.mean(moved * moved, axis=-1, keepdims=True)
    normal = moved * lax.rsqrt(spread + 1e-06)
    return (normal * (1.0 + scale) + shift).astype(BF16)


def qk_normalize(heads, gain):
    factor = lax.rsqrt(jnp.mean(heads * heads, axis=1, keepdims=True) + 1e-06)
    return heads * factor * gain[None]


def pad_rows(heads, fill):
    n, _, tokens = heads.shape
    return jnp.concatenate([heads, jnp.full((n, 8, tokens), fill, F32)], axis=1)


def nt_dot(a, b):
    return lax.dot_general(a, b, (((1,), (1,)), ((), ())), preferred_element_type=F32)


def tn_dot(a, b):
    return lax.dot_general(a, b, (((0,), (0,)), ((), ())), preferred_element_type=F32)


def block_kernel(frames, modulation_in, gains_in, w_qkv, w_out, w_qkv_two, w_out_two, home,
                 modulation, gains_raw, gains, xbuf, raw, wt, wt_two, wo, wo_two, q_t, k_rows, v_t, o_t, att, att2, fr2, res, perm, bias,
                 m_sem, w_sem, x_send, x_recv, x_fwd, kv_send, kv_recv, a_send, a_recv, f_send, f_recv, r_send, r_recv, stages,
                 *, exact):
    f_me = lax.axis_index("frame")
    s_me = lax.axis_index("seq")
    group, core = f_me // 2, f_me % 2
    x_lo, y = s_me // 4, s_me % 4
    half = lax.rem(y, 2)
    frame = 4 * group + 2 * x_lo + y // 2
    partner = 2 * group + 1 - core
    mate_row = y + 1 - 2 * half
    same = x_lo == core

    def raw_copy(part):
        return pltpu.make_async_copy(
            w_qkv.at[:, pl.ds(pl.multiple_of(part * D + half * 512, 128), 640)],
            raw.at[part, :, pl.ds(0, 640)], w_sem.at[part])

    def raw_copy_two(part):
        return pltpu.make_async_copy(w_qkv_two.at[:, pl.ds(pl.multiple_of(part * D, 128), D)], raw.at[part], w_sem.at[part])

    small_copies = [pltpu.make_async_copy(modulation_in, modulation, m_sem.at[0]),
                    pltpu.make_async_copy(gains_in, gains_raw, m_sem.at[1])]
    out_copies = [pltpu.make_async_copy(w_out, wo, w_sem.at[3]), pltpu.make_async_copy(w_out_two, wo_two, w_sem.at[4])]

    barrier = pltpu.get_barrier_semaphore()

    def plane_mate(n):
        step = n + 1
        return (2 * group + lax.rem(core + lax.rem(step, 2), 2),
                4 * lax.rem(x_lo + lax.rem(step // 2, 2), 2) + lax.rem(y + step // 4, 4))

    above, below = (lax.rem(f_me + 4, 16), s_me), (lax.rem(f_me + 12, 16), s_me)
    beside = (f_me + 2 - 4 * lax.rem(f_me // 2, 2), 4 * (1 - x_lo) + y)

    def tell(sem, mate):
        pl.semaphore_signal(sem, inc=1, device_id=mate, device_id_type=MESH)

    for n in range(15):
        tell(barrier, plane_mate(n))
    for mate in (above, below, beside):
        tell(barrier, mate)
    for part in range(3):
        raw_copy(part).start()
    pl.semaphore_wait(barrier, 18)

    def across(i):
        return lax.rem(i + y // 2, 2)

    def send(i):
        return pltpu.make_async_remote_copy(
            src_ref=frames.at[i], dst_ref=xbuf.at[y], send_sem=x_send.at[i], recv_sem=x_recv.at[y],
            device_id=(2 * group + x_lo, 4 * core + y + across(i) * (3 - 2 * y)), device_id_type=MESH)

    def forward(slot):
        return pltpu.make_async_remote_copy(
            src_ref=xbuf.at[slot], dst_ref=xbuf.at[slot], send_sem=x_fwd.at[slot], recv_sem=x_recv.at[slot],
            device_id=(f_me, 4 * x_lo + mate_row), device_id_type=MESH)

    for i in range(2):
        @pl.when((across(i) == 0) & jnp.logical_not(same))
        def _(i=i):
            send(i).start()

        @pl.when((across(i) == 0) & same)
        def _(i=i):
            pltpu.make_async_copy(frames.at[i], xbuf.at[y], x_recv.at[y]).start()

        @pl.when((across(i) == 1) & same)
        def _(i=i):
            send(i).start()

    for mate in (above, below):
        tell(stages.at[0], mate)
    for copy in small_copies:
        copy.start()
    for copy in out_copies:
        copy.start()

    def receive(slot):
        pltpu.make_async_copy(frames.at[0], xbuf.at[slot], x_recv.at[slot]).wait()

    receive(y)
    forward(y).start()
    for i in range(2):
        @pl.when((across(i) == 1) & jnp.logical_not(same))
        def _(i=i):
            send(1 - i).wait_send()
            send(i).start()

    for copy in small_copies:
        copy.wait()
    diagonal = lax.broadcasted_iota(jnp.int32, (HD, HD), 0) == lax.broadcasted_iota(jnp.int32, (HD, HD), 1)
    for layer in range(2):
        for which in range(2):
            gains[layer, which] = jnp.sum(
                jnp.where(diagonal, gains_raw[layer, which:which + 1, :], 0.0), axis=1, keepdims=True)
    for part in range(3):
        raw_copy(part).wait()
        wt[part] = raw[part, :, :640].T
        raw_copy_two(part).start()

    scale, shift = modulation[1, 0:1, :], modulation[0, 0:1, :]
    weight_rows = pl.ds(pl.multiple_of(half * 64, 64), HALF)

    def row_of(n):
        row = y + (n // 2) * (mate_row - y)
        return row + lax.rem(n, 2) * (3 - 2 * row)

    pl.semaphore_wait(stages.at[0], 2)
    tell(stages.at[1], above)

    def k_copy(n):
        cols = pl.ds(pl.multiple_of(n * 512 + core * 256, 256), 256)
        return pltpu.make_async_remote_copy(
            src_ref=k_rows.at[:, cols], dst_ref=k_rows.at[:, cols], send_sem=kv_send.at[0, n],
            recv_sem=kv_recv.at[0, n], device_id=(partner, s_me), device_id_type=MESH)

    def v_copy(n):
        cols = pl.ds(pl.multiple_of(n * 512 + core * 256, 256), 256)
        return pltpu.make_async_remote_copy(
            src_ref=v_t.at[:, :, cols], dst_ref=v_t.at[:, :, cols], send_sem=kv_send.at[1, n],
            recv_sem=kv_recv.at[1, n], device_id=(partner, s_me), device_id_type=MESH)

    def kv_wait(n):
        cols = pl.ds(pl.multiple_of(n * 512 + (1 - core) * 256, 256), 256)
        pltpu.make_async_copy(k_rows.at[:, cols], k_rows.at[:, cols], kv_recv.at[0, n]).wait()
        pltpu.make_async_copy(v_t.at[:, :, cols], v_t.at[:, :, cols], kv_recv.at[1, n]).wait()

    def work(n):
        values = xbuf[row_of(n)].astype(F32).reshape(16, 2, 8, D)
        values = jnp.concatenate([values[:, 0].reshape(128, D), values[:, 1].reshape(128, D)], axis=0)
        normed = layer_norm(values, scale, shift)
        cols = pl.ds(pl.multiple_of(n * 512 + core * 256, 256), 256)

        def projected(part):
            return nt_dot(wt[part, weight_rows, :], normed).astype(BF16).astype(F32).reshape(8, HD, 256)

        keys = pad_rows(qk_normalize(projected(1), gains[0, 1]), 1.0)
        for h in range(8):
            k_rows[h, cols, :] = keys[h].T.astype(BF16)
        k_copy(n).start()
        v_t[:, :, cols] = pad_rows(projected(2), 1.0).astype(BF16)
        v_copy(n).start()
        queries = pad_rows(qk_normalize(projected(0), gains[0, 0]), -6.0).astype(BF16)
        q_t[:, :, pl.ds(pl.multiple_of(n * 128, 128), 128)] = queries[:, :, :128]
        q_t[:, :, pl.ds(pl.multiple_of(512 + n * 128, 128), 128)] = queries[:, :, 128:]

    work(0)
    pl.semaphore_wait(stages.at[1], 1)
    tell(stages.at[2], beside)


    my_rows = pl.ds(pl.multiple_of(f_me * 16, 16), 16)

    def near(n):
        step = 15 - n
        z = lax.rem(f_me // 4 + lax.rem(step, 4), 4)
        x_hi = lax.rem(f_me // 2 + step // 4, 2)
        return 4 * z + 2 * x_hi + lax.rem(core + step // 8, 2)

    def send_frame(n, carry):
        other = near(n)
        rows = pl.ds(pl.multiple_of(other * 16, 16), 16)
        pltpu.make_async_remote_copy(
            src_ref=frames.at[:, rows], dst_ref=fr2.at[pl.ds(2 * f_me, 2)], send_sem=f_send, recv_sem=f_recv,
            device_id=(other, s_me), device_id_type=MESH).start()
        return carry


    def chunk(n, carry):
        slot = row_of(n)
        receive(slot)

        @pl.when(n == 1)
        def _():
            forward(slot).start()

        work(n)
        raw_copy_two(n - 1).wait()
        wt_two[n - 1] = raw[n - 1].T
        return carry

    pl.semaphore_wait(stages.at[2], 1)
    lax.fori_loop(4, 8, send_frame, 0)
    lax.fori_loop(12, 15, send_frame, 0)
    lax.fori_loop(1, 3, chunk, 0)
    raw_copy_two(2).wait()
    wt_two[2] = raw[2].T

    row = lax.broadcasted_iota(jnp.int32, (256, 256), 0)
    column = lax.broadcasted_iota(jnp.int32, (256, 256), 1)
    perm[...] = jnp.where(column == (row & 31) * 8 + (row >> 5), 1.0, 0.0).astype(BF16)
    bias[...] = jnp.where((row >> 5) == (column >> 5), 0.0, -1e30)

    def finish(summed):
        return summed[:HD] / summed[HD:HD + 1]

    lax.fori_loop(0, 4, send_frame, 0)
    lax.fori_loop(8, 12, send_frame, 0)
    pltpu.make_async_copy(frames.at[:, my_rows], fr2.at[pl.ds(2 * f_me, 2)], f_recv).start()
    receive(row_of(3))
    work(3)
    for n in range(4):
        kv_wait(n)

    def attend(block):
        cols = slice(block * 512, block * 512 + 512)

        def head(h, carry):
            scores = jnp.dot(k_rows[h], q_t[h, :, cols], preferred_element_type=F32)
            if exact:
                scores = scores - jnp.max(scores, axis=0, keepdims=True)
            weights = jnp.exp2(scores * SCALE).astype(BF16)
            o_t[h, :, cols] = finish(jnp.dot(v_t[h], weights, preferred_element_type=F32))
            return carry

        lax.fori_loop(0, 8, head, 0, unroll=2)
        for part in range(4):
            cols = slice(block * 512 + part * 128, block * 512 + part * 128 + 128)
            rows = o_t[:, :, cols].reshape(HALF, 128).T.reshape(16, 8, HALF)
            att[block * 64 + part * 16:block * 64 + part * 16 + 16] = rows.astype(BF16)

        def send_att(n, carry):
            part = n // 32 + lax.rem(n, 2) * (3 - 2 * (n // 32))
            i = row_of(part)
            owner = near(lax.rem(n // 2, 16))
            block_ref = att.at[block * 64 + part * 16 + owner]
            mine = (owner == f_me) & (4 * core + i == s_me)

            @pl.when(jnp.logical_not(mine))
            def _():
                pltpu.make_async_remote_copy(
                    src_ref=block_ref, dst_ref=att2.at[block, half, frame], send_sem=a_send, recv_sem=a_recv.at[block],
                    device_id=(owner, 4 * core + i), device_id_type=MESH).start()

            @pl.when(mine)
            def _():
                pltpu.make_async_copy(block_ref, att2.at[block, half, frame], a_recv.at[block]).start()
            return carry

        lax.fori_loop(0, 64, send_att, 0)

    for block in range(2):
        attend(block)

    for i in range(2):
        @pl.when(across(i) == 1)
        def _(i=i):
            send(i).wait_send()

    forward(y).wait_send()
    forward(3 - y).wait_send()

    for slot in range(4):
        k_copy(slot).wait_send()
        v_copy(slot).wait_send()
    for copy in out_copies:
        copy.wait()
    pltpu.make_async_copy(fr2, fr2, f_recv).wait()

    def temporal(turn, carry):
        pltpu.make_async_copy(att2.at[turn], att2.at[turn], a_recv.at[turn]).wait()
        branch = jnp.zeros((256, D), F32)
        for hh in range(2):
            rows = att2[turn, hh].astype(F32).reshape(256, HALF).astype(BF16)
            branch = branch + jnp.dot(rows, wo[HALF * hh:HALF * hh + HALF], preferred_element_type=F32)
        rows = fr2[...].astype(F32).reshape(32, 2, 8, D)
        rows = jnp.where(turn == 0, rows[:, 0], rows[:, 1]).reshape(256, D)
        stream = (rows + modulation[2, 0:1, :] * branch).astype(BF16)
        normed = layer_norm(stream.astype(F32), modulation[1, 1:2, :], modulation[0, 1:2, :])
        normed = jnp.dot(perm[...], normed, preferred_element_type=F32).astype(BF16)

        def projected_two(part):
            return nt_dot(wt_two[part], normed).astype(BF16).astype(F32).reshape(HEADS, HD, 256)

        keys = pad_rows(qk_normalize(projected_two(1), gains[1, 1]), 1.0)
        queries = pad_rows(qk_normalize(projected_two(0), gains[1, 0]), -6.0).astype(BF16)
        values = pad_rows(projected_two(2), 1.0).astype(BF16)
        for h in range(HEADS):
            cols = pl.ds(256 * (h % 4), 256)
            k_rows[h // 4, cols, :] = keys[h].T.astype(BF16)
            q_t[h // 4, :, cols] = queries[h]
            v_t[h // 4, :, cols] = values[h]

        def four_heads(h, carry):
            parts = [slice(part * 256, part * 256 + 256) for part in range(4)]
            scores = [jnp.dot(k_rows[h, cols, :], q_t[h, :, cols], preferred_element_type=F32) for cols in parts]
            if exact:
                scores = [each - jnp.max(each + bias[...], axis=0, keepdims=True) for each in scores]
            weights = [jnp.exp2(each * SCALE + bias[...]).astype(BF16) for each in scores]
            summed = [jnp.dot(v_t[h, :, cols], each, preferred_element_type=F32) for cols, each in zip(parts, weights)]
            for cols, each in zip(parts, summed):
                o_t[h, :, cols] = finish(each)
            return carry

        lax.fori_loop(0, 4, four_heads, 0)
        attended = jnp.concatenate([o_t[h // 4, :, 256 * (h % 4):256 * (h % 4) + 256] for h in range(HEADS)], axis=0)
        attended = jnp.dot(attended.astype(BF16), perm[...], preferred_element_type=F32).astype(BF16)
        result = stream.astype(F32) + modulation[2, 1:2, :] * tn_dot(attended, wo_two[...])
        res[turn] = result.reshape(32, 8, D).astype(BF16)

        def send_home(n, carry):
            other = near(n)
            pltpu.make_async_remote_copy(
                src_ref=res.at[turn, pl.ds(2 * other, 2)], dst_ref=home.at[f_me, turn], send_sem=r_send, recv_sem=r_recv,
                device_id=(other, s_me), device_id_type=MESH).start()
            return carry

        lax.fori_loop(0, 15, send_home, 0)
        pltpu.make_async_copy(res.at[turn, pl.ds(2 * f_me, 2)], home.at[f_me, turn], r_recv).start()
        return carry

    lax.fori_loop(0, 2, temporal, 0)

    @pl.when(same)
    def _():
        part = att.at[pl.ds(0, 126)]
        pltpu.make_async_copy(part, part, a_send).wait()

    @pl.when(jnp.logical_not(same))
    def _():
        pltpu.make_async_copy(att, att, a_send).wait()
    most = fr2.at[pl.ds(0, 30)]
    pltpu.make_async_copy(most, most, f_send).wait()
    most = res.at[:, pl.ds(0, 30)]
    pltpu.make_async_copy(most, most, r_send).wait()
    pltpu.make_async_copy(home, home, r_recv).wait()


def block_call(exact, frames, modulation, gains, w_qkv, w_out, w_qkv_two, w_out_two):
    anywhere = pl.BlockSpec(memory_space=pl.ANY)
    dma = pltpu.SemaphoreType.DMA
    return pl.pallas_call(
        functools.partial(block_kernel, exact=exact),
        out_shape=jax.ShapeDtypeStruct((16, 2, 2, 8, D), BF16),
        in_specs=[anywhere, anywhere, anywhere, anywhere, anywhere, anywhere, anywhere],
        out_specs=anywhere,
        scratch_shapes=[
            pltpu.VMEM((3, 2, D), F32),
            pltpu.VMEM((2, 2, HD), F32),
            pltpu.VMEM((2, 2, HD, 1), F32),
            pltpu.VMEM((4, 256, D), BF16),
            pltpu.VMEM((3, D, D), BF16),
            pltpu.VMEM((3, 640, D), BF16),
            pltpu.VMEM((3, D, D), BF16),
            pltpu.VMEM((D, D), BF16),
            pltpu.VMEM((D, D), BF16),
            pltpu.VMEM((8, 80, 1024), BF16),
            pltpu.VMEM((8, 2048, 80), BF16),
            pltpu.VMEM((8, 80, 2048), BF16),
            pltpu.VMEM((8, HD, 1024), F32),
            pltpu.VMEM((128, 8, HALF), BF16),
            pltpu.VMEM((2, 2, 32, 8, HALF), BF16),
            pltpu.VMEM((32, 16, D), BF16),
            pltpu.VMEM((2, 32, 8, D), BF16),
            pltpu.VMEM((256, 256), BF16),
            pltpu.VMEM((256, 256), F32),
            dma((2,)), dma((5,)), dma((2,)), dma((4,)), dma((4,)), dma((2, 4)), dma((2, 4)),
            dma, dma((2,)), dma, dma, dma, dma, pltpu.SemaphoreType.REGULAR((3,)),
        ],
        compiler_params=pltpu.CompilerParams(
            collective_id=1 if exact else 0, has_side_effects=True, vmem_limit_bytes=60 << 20),
        name="block_exact" if exact else "block",
    )(frames, modulation, gains, w_qkv, w_out, w_qkv_two, w_out_two)


def body(frames, modulation, spatial_qkv, spatial_out, temporal_qkv, temporal_out, qk_gain):
    largest = jnp.max(jnp.abs(qk_gain[:, 0] * qk_gain[:, 1]))
    home = lax.cond(
        largest <= 115.0 / (72.0 * SCALE), functools.partial(block_call, False), functools.partial(block_call, True),
        frames, jnp.transpose(modulation, (1, 0, 2)), qk_gain, spatial_qkv, spatial_out, temporal_qkv, temporal_out)
    return jnp.transpose(home, (2, 0, 1, 3, 4)).reshape(2, 256, D)


def solution(mesh):
    in_specs = (P("frame", "seq", None), P(), P(), P(), P(), P(), P())
    out_specs = P("frame", "seq", None)
    return jax.shard_map(body, mesh=mesh, in_specs=in_specs, out_specs=out_specs, check_vma=False)
```
